128 devices in a mesh: prefix: 8 (over z, core), seq: 16 (over x, y).
Axes of the slice: x: 4, y: 4, z: 4, core: 2. Of those that a mesh axis runs over, the one named last changes fastest.
Arguments:
- queries: bfloat16 [1024, 4, 8192], P(('prefix', 'seq')), may hold values from -28 to 28
- new_keys: bfloat16 [1024, 4, 1024], P(('prefix', 'seq')), may hold values from -24 to 24
- new_values: bfloat16 [1024, 4, 1024], P(('prefix', 'seq')), may hold values from -6 to 6
- suffix_keys: bfloat16 [1024, 256, 1024], P(('prefix', 'seq')), may hold values from -24 to 24
- suffix_values: bfloat16 [1024, 256, 1024], P(('prefix', 'seq')), may hold values from -6 to 6
- suffix_len: int32 [1024], P(('prefix', 'seq')), may hold values from 1 to 256, 131072 in all
- row_prefix: int32 [1024, 1], P(('prefix', 'seq')), may hold values from 0 to 7; in each aligned block of 8 rows (0 to 7, 8 to 15, ...) at most 2 rows name the same one
- prefix_key_codes: bfloat16 [8, 12288, 1024], P('prefix', 'seq'), may hold values from -48 to 48
- prefix_value_codes: bfloat16 [8, 12288, 1024], P('prefix', 'seq'), may hold values from -6 to 6
- scale_index: int32 [8, 96, 8], P('prefix', 'seq'), may hold values from 0 to 255
- scale_table: float32 [2, 256], replicated, may hold values from 0.5 to 2, as said below
Outputs:
- attended: bfloat16 [1024, 4, 8192], P(('prefix', 'seq'))
The draws below stay inside these ranges and needn't reach their ends.
Inputs may be any that keep to these rules, and one draw needn't show every extreme that they name: `row_prefix`: among the rows of one device, at most 2 name any one prefix, a bound that some block reaches of them. `scale_table`: every entry is 0.5, 1 or 2.
All inputs are finite; a program needn't handle non-finite values. No bound on the sum of `suffix_len` on one device may be relied on, other than what follows from the above.
Results may differ from the reference program's by a relative error of at most 0.0046.
Values may be sent and summed in bfloat16 or wider, within the bound.
No kernel may reach another device: no remote copies, remote signals or barrier semaphores. Data moves between devices by JAX's collectives and lax.ppermute only.
A program may use at most 256 MiB of HBM per device.

```python
import math
import jax
import jax.numpy as jnp
import numpy as np
from jax import lax

QH = 64
KVH = 8
HD = 128
STEPS = 4
BLOCK = 128
SCALES = 256
ROWS_DEV = 8
PFX_DEV = 768
SUF_MAX = 256
CAP = 2
PREFIXES = 8
PREFIX_LEN = 12288
ROWS = 1024
N_SEQ = 16


def table_powers(key):
    return jax.random.randint(jax.random.fold_in(key, 103), (2, SCALES), -1, 2)


def block_entries(key):
    return jax.random.randint(jax.random.fold_in(key, 104), (PREFIXES, PREFIX_LEN // BLOCK, KVH), 0, SCALES)


def token_key_scales(key):
    table = jnp.exp2(table_powers(key)[0].astype(jnp.float32))
    picked = jnp.take(table, block_entries(key))
    return jnp.repeat(picked, BLOCK, axis=1)


def row_common(key):
    return jnp.clip(jax.random.normal(jax.random.fold_in(key, 201), (ROWS, KVH, HD), jnp.float32), -4.0, 4.0)


def local_boost():
    return math.log(PREFIX_LEN / (SUF_MAX // 2 + STEPS))


def draw_scale_table(key, part):
    powers = table_powers(key)
    return jnp.exp2(powers.astype(jnp.float32))


def draw_scale_index(key, part):
    entries = block_entries(key)
    return entries.astype(jnp.int32)


def draw_queries(key, part):
    common = row_common(key)
    key = jax.random.fold_in(key, 1)
    shape = (ROWS, STEPS, KVH, QH // KVH, HD)
    base = 1.2 * jax.random.normal(key, shape, jnp.float32)
    base = base + common[:, None, :, None, :]
    base = jnp.clip(base, -28.0, 28.0)
    return base.reshape(ROWS, STEPS, QH * HD).astype(jnp.bfloat16)


def draw_suffix_keys(key, part):
    common = row_common(key)
    key = jax.random.fold_in(key, 5)
    shape = (ROWS, SUF_MAX, KVH, HD)
    base = jnp.clip(jax.random.normal(key, shape, jnp.float32), -6.0, 6.0)
    base = base + local_boost() / math.sqrt(HD) * common[:, None, :, :]
    base = jnp.clip(base, -24.0, 24.0)
    return base.reshape(ROWS, SUF_MAX, KVH * HD).astype(jnp.bfloat16)


def draw_new_keys(key, part):
    common = row_common(key)
    key = jax.random.fold_in(key, 6)
    shape = (ROWS, STEPS, KVH, HD)
    base = jnp.clip(jax.random.normal(key, shape, jnp.float32), -6.0, 6.0)
    base = base + (local_boost() + 2.5) / math.sqrt(HD) * common[:, None, :, :]
    base = jnp.clip(base, -24.0, 24.0)
    return base.reshape(ROWS, STEPS, KVH * HD).astype(jnp.bfloat16)


def draw_prefix_key_codes(key, part):
    scales = token_key_scales(key)
    key = jax.random.fold_in(key, 3)
    shape = (PREFIXES, PREFIX_LEN, KVH, HD)
    base = jnp.clip(jax.random.normal(key, shape, jnp.float32), -6.0, 6.0)
    codes = base / scales[..., None]
    codes = jnp.clip(codes, -48.0, 48.0)
    return codes.reshape(PREFIXES, PREFIX_LEN, KVH * HD).astype(jnp.bfloat16)


def block_levels(rng, dims, pieces, least, largest):
    factor_of, own = 1.0, jax.random.fold_in(rng, 6)
    for dim, parts in pieces:
        draws = jnp.exp(jax.random.uniform(jax.random.fold_in(own, dim), (parts,), jnp.float32, least / len(pieces), largest / len(pieces)))
        factor_of = factor_of * jnp.repeat(draws, dims[dim] // parts).reshape([-1 if axis == dim else 1 for axis in range(len(dims))])
    return factor_of


def length_profile(count, total, reach, skew):
    loads = [(1 << 20) // math.isqrt(grade ** skew) + 1 for grade in range(2, count + 1)]
    rest, given = total - reach - (count - 1), [1] * (count - 1)
    while rest > 0:
        movable = [i for i in range(count - 1) if given[i] < reach]
        pool, remaining = sum([loads[i] for i in movable]), rest
        for i in movable:
            more = min(reach - given[i], max(1, remaining * loads[i] // pool), rest)
            given[i] = given[i] + more
            rest = rest - more
    return np.array([reach] + given)


def ragged(own_key, amount, total, reach, skew):
    if amount == 2:
        one = jax.random.randint(own_key, (), max(1, total - reach), min(reach, total - 1) + 1)
        return jnp.stack([one, total - one])
    lengths = jnp.asarray(length_profile(amount, total, reach, skew), jnp.int32)
    couples = (amount - 1) // 2
    giver, receiver = lengths[1:1 + 2 * couples:2], lengths[2:2 + 2 * couples:2]
    slack = jnp.minimum(giver - 1, reach - receiver)
    shifted = jax.random.randint(jax.random.fold_in(own_key, 1), (couples,), 0, 1 << 20) % (slack + 1)
    lengths = lengths.at[1:1 + 2 * couples:2].set(giver - shifted).at[2:2 + 2 * couples:2].set(receiver + shifted)
    return lengths[jax.random.permutation(jax.random.fold_in(own_key, 2), amount)]


def shared_out(own_key, own, number, rows, count, top, bound, slope):
    ranking = jax.random.permutation(own_key, count)
    crowded, usual = shares(count, rows * top, bound, slope, True), shares(count, rows * top, bound, slope, False)
    places = jnp.arange(count)

    def named(lengths, offset_by):
        used = int((lengths > 0).sum())
        fixed = max(1, used // 4)
        moved = fixed + (places - fixed + offset_by * (used - fixed)) % max(1, count - fixed)
        return jnp.zeros((count,), jnp.int32).at[ranking[jnp.where(places < fixed, places, moved)]].set(jnp.asarray(lengths, jnp.int32))

    lengths = jnp.where(number % 4 == 0, named(crowded, number // 4), named(usual, number - number // 4 - 1))
    mixed = jax.random.permutation(jax.random.fold_in(own, 3), count)
    source_of, taker = mixed[0:count // 2 * 2:2], mixed[1:count // 2 * 2:2]
    slack = jnp.minimum(lengths[source_of] - 1, bound - lengths[taker]) // 2
    slack = jnp.where((source_of == ranking[0]) | (taker == ranking[0]) | (lengths[taker] == 0), 0, jnp.maximum(slack, 0))
    moved = jax.random.randint(jax.random.fold_in(own, 4), (count // 2,), 0, 1 << 20) % (slack + 1)
    lengths = lengths.at[source_of].add(-moved).at[taker].add(moved)
    members = jnp.searchsorted(jnp.cumsum(lengths), jnp.arange(rows * top), side="right").astype(jnp.int32)
    table = members.reshape(top, rows).T
    table = table[jax.random.permutation(jax.random.fold_in(own, 1), rows)]
    offset_by = jax.random.randint(jax.random.fold_in(own, 2), (rows, 1), 0, top)
    return jnp.take_along_axis(table, (jnp.arange(top)[None, :] + offset_by) % top, axis=1)


def shares(count, total, reach, skew, full):
    loads = [(1 << 20) // math.isqrt(rank ** skew) + 1 for rank in range(1, count + 1)]
    largest = reach if full else min(reach, max(-(-total // count), total * loads[0] // sum(loads)))
    least = 1 if total - largest >= count - 1 else 0
    given, surplus = [largest] + [least] * (count - 1), total - largest - least * (count - 1)
    while surplus > 0:
        candidates = [i for i in range(1, count) if given[i] < largest] or [i for i in range(1, count) if given[i] < reach]
        mass, remaining = sum([loads[i] for i in candidates]), surplus
        for i in candidates:
            extra = min(reach - given[i], max(1, remaining * loads[i] // mass), surplus)
            given[i] = given[i] + extra
            surplus = surplus - extra
    return np.array(given)


def normal_values(own_key, extent, spread, limit, shards=(), kind=jnp.bfloat16):
    values = spread * jax.random.normal(own_key, extent, jnp.float32)
    if shards:
        values = values * block_levels(own_key, extent, shards, -0.22, 0.18)
    return jnp.clip(values, -limit, limit).astype(kind)


def setup_inputs(seed: int = 0) -> dict:
    arg_keys = jax.random.split(jax.random.key(seed), 12)
    queries = draw_queries(jax.random.fold_in(arg_keys[11], 71), 0)
    new_keys = draw_new_keys(jax.random.fold_in(arg_keys[11], 71), 0)
    new_values = normal_values(arg_keys[2], (ROWS, STEPS, KVH * HD), 1.0, 6.0, ((0, 128),))
    suffix_keys = draw_suffix_keys(jax.random.fold_in(arg_keys[11], 71), 0)
    suffix_values = normal_values(arg_keys[4], (ROWS, SUF_MAX, KVH * HD), 1.0, 6.0, ((0, 128),))
    suffix_len = ragged(arg_keys[5], ROWS, ROWS * SUF_MAX // 2, SUF_MAX, 2).astype(jnp.int32)
    row_prefix_keys = jax.random.split(jax.random.fold_in(arg_keys[6], 1), ROWS // ROWS_DEV)
    row_prefix_turns = jax.random.permutation(jax.random.fold_in(arg_keys[6], 3), ROWS // ROWS_DEV)
    row_prefix = jax.vmap(lambda own, number: shared_out(jax.random.fold_in(arg_keys[6], 2), own, number, ROWS_DEV, PREFIXES, 1, CAP, 2))(row_prefix_keys, row_prefix_turns).reshape((ROWS, 1))
    prefix_key_codes = draw_prefix_key_codes(jax.random.fold_in(arg_keys[11], 71), 0)
    prefix_value_codes = normal_values(arg_keys[8], (PREFIXES, PREFIX_LEN, KVH * HD), 1.0, 6.0, ((0, 8), (1, 16)))
    scale_index = draw_scale_index(jax.random.fold_in(arg_keys[11], 71), 0)
    scale_table = draw_scale_table(jax.random.fold_in(arg_keys[11], 71), 0)
    return dict(queries=queries, new_keys=new_keys, new_values=new_values, suffix_keys=suffix_keys, suffix_values=suffix_values, suffix_len=suffix_len, row_prefix=row_prefix, prefix_key_codes=prefix_key_codes, prefix_value_codes=prefix_value_codes, scale_index=scale_index, scale_table=scale_table)


SCORE_FLOOR = -1e30


def reference(queries, new_keys, new_values, suffix_keys, suffix_values, suffix_len, row_prefix, prefix_key_codes, prefix_value_codes, scale_index, scale_table):
    group = QH // KVH
    factor = HD ** -0.5
    key_scales = jnp.repeat(scale_table[0][scale_index], BLOCK, axis=1)
    value_scales = jnp.repeat(scale_table[1][scale_index], BLOCK, axis=1)
    keys_all = (prefix_key_codes.reshape(PREFIXES, PREFIX_LEN, KVH, HD).astype(jnp.float32) * key_scales[..., None]).astype(jnp.bfloat16)
    values_all = (prefix_value_codes.reshape(PREFIXES, PREFIX_LEN, KVH, HD).astype(jnp.float32) * value_scales[..., None]).astype(jnp.bfloat16)
    position = jnp.arange(SUF_MAX + STEPS, dtype=jnp.int32)
    step_ids = jnp.arange(STEPS, dtype=jnp.int32)

    def one_row(index):
        target = row_prefix[index, 0]
        query = queries[index].reshape(STEPS, KVH, group, HD).astype(jnp.float32)
        keys = lax.dynamic_index_in_dim(keys_all, target, 0, keepdims=False).reshape(N_SEQ, PFX_DEV, KVH, HD).astype(jnp.float32)
        values = lax.dynamic_index_in_dim(values_all, target, 0, keepdims=False).reshape(N_SEQ, PFX_DEV, KVH, HD).astype(jnp.float32)
        scores = jnp.einsum("tkgd,spkd->stkgp", query, keys) * factor
        highest = jnp.max(scores, axis=-1, keepdims=True)
        exponent = jnp.exp(scores - highest)
        totals = jnp.sum(exponent, axis=-1, keepdims=True)
        weights = lax.optimization_barrier(exponent.astype(jnp.bfloat16)).astype(jnp.float32)
        numerator = jnp.einsum("stkgp,spkd->stkgd", weights, values)
        shard_outs = lax.optimization_barrier((numerator / totals).astype(jnp.bfloat16)).astype(jnp.float32)
        shard_lses = highest[..., 0] + jnp.log(totals[..., 0])
        best = jnp.max(shard_lses, axis=0, keepdims=True)
        scaled = jnp.exp(shard_lses - best)
        denominator = jnp.sum(scaled, axis=0)
        prefix_out = jnp.sum(scaled[..., None] * shard_outs, axis=0) / denominator[..., None]
        prefix_out = lax.optimization_barrier(prefix_out.astype(jnp.bfloat16)).astype(jnp.float32)
        prefix_lse = best[0] + jnp.log(denominator)
        local_keys = jnp.concatenate([suffix_keys[index].reshape(SUF_MAX, KVH, HD), new_keys[index].reshape(STEPS, KVH, HD)], axis=0).astype(jnp.float32)
        local_values = jnp.concatenate([suffix_values[index].reshape(SUF_MAX, KVH, HD), new_values[index].reshape(STEPS, KVH, HD)], axis=0).astype(jnp.float32)
        visible = jnp.where(position[None, :] < SUF_MAX, position[None, :] < suffix_len[index], (position[None, :] - SUF_MAX) <= step_ids[:, None])
        local_scores = jnp.einsum("tkgd,jkd->tkgj", query, local_keys) * factor
        local_scores = jnp.where(visible[:, None, None, :], local_scores, SCORE_FLOOR)
        local_high = jnp.max(local_scores, axis=-1, keepdims=True)
        local_exp = jnp.exp(local_scores - local_high)
        local_total = jnp.sum(local_exp, axis=-1, keepdims=True)
        local_weights = lax.optimization_barrier(local_exp.astype(jnp.bfloat16)).astype(jnp.float32)
        local_out = jnp.einsum("tkgj,jkd->tkgd", local_weights, local_values) / local_total
        local_lse = local_high[..., 0] + jnp.log(local_total[..., 0])
        joint = jnp.maximum(local_lse, prefix_lse)
        local_share = jnp.exp(local_lse - joint)
        prefix_share = jnp.exp(prefix_lse - joint)
        result = (local_share[..., None] * local_out + prefix_share[..., None] * prefix_out) / (local_share + prefix_share)[..., None]
        return result.reshape(STEPS, QH * HD).astype(jnp.bfloat16)

    return lax.map(one_row, jnp.arange(ROWS, dtype=jnp.int32))
```

```python
import functools
import math

import jax
import jax.numpy as jnp
from jax import lax
from jax.experimental import pallas as pl
from jax.experimental.pallas import tpu as pltpu
from jax.sharding import PartitionSpec as P

QH = 64
KVH = 8
HD = 128
STEPS = 4
BLOCK = 128
GROUP = QH // KVH
QROWS = GROUP * STEPS
SLOTS = 2
CHUNKS = 4
TQ = 512
EXTRA = 8
SCALE = HD**-0.5
SCALE2 = SCALE * math.log2(math.e)
LN2 = math.log(2.0)
FLOOR = -1e30
NT = (((1,), (1,)), ((), ()))
MIB = 2**20


def arrange(rows):
    wide = rows.astype(jnp.float32)
    heads = []
    for k in range(KVH):
        parts = [wide[:, (k * GROUP + g) * HD : (k * GROUP + g + 1) * HD] for g in range(GROUP)]
        heads.append(jnp.concatenate(parts, axis=0))
    return heads


def row_in_slot(names, prefix, slot, rows):
    found, seen = jnp.int32(-1), jnp.int32(0)
    for r in range(rows):
        hit = names[r] == prefix
        found = jnp.where(jnp.logical_and(hit, seen == slot), r, found)
        seen = seen + hit.astype(jnp.int32)
    return found


def slot_of_row(names, row, rows):
    prefix = names[row]
    seen = jnp.int32(0)
    for r in range(rows):
        earlier = jnp.logical_and(names[r] == prefix, r < row)
        seen = seen + earlier.astype(jnp.int32)
    return prefix, seen


def slot_coords(j):
    return (j // 4) * 2 + j % 2, (j // 2) % 2


def outgoing_kernel(rows, names, q_ref, o_ref):
    prefix, slot = slot_coords(pl.program_id(0))
    filled = row_in_slot(names, prefix, slot, rows) >= 0
    heads = arrange(q_ref[0])
    for k in range(KVH):
        o_ref[0, k] = jnp.where(filled, heads[k], 0.0).astype(jnp.bfloat16)


def outgoing_queries(names, queries):
    rows = queries.shape[0]
    slots = 8 * SLOTS

    def pick(j, names):
        prefix, slot = slot_coords(j)
        return (jnp.maximum(row_in_slot(names, prefix, slot, rows), 0), 0, 0)

    return pl.pallas_call(
        functools.partial(outgoing_kernel, rows),
        grid_spec=pltpu.PrefetchScalarGridSpec(
            num_scalar_prefetch=1,
            grid=(slots,),
            in_specs=[pl.BlockSpec((1, STEPS, QH * HD), pick)],
            out_specs=pl.BlockSpec((1, KVH, QROWS, HD), lambda j, names: (j, 0, 0, 0)),
        ),
        out_shape=jax.ShapeDtypeStruct((slots, KVH, QROWS, HD), jnp.bfloat16),
        cost_estimate=pl.CostEstimate(flops=0, bytes_accessed=2 * MIB, transcendentals=0),
    )(names, queries)


def prepare_kernel(core_ref, index_ref, table_ref, k_ref, v_ref, *outs):
    head = pl.program_id(0)
    core = core_ref[0]
    keeps, sends = outs[:-1], outs[-1]
    part = keeps[0].shape[2]
    half = part * CHUNKS
    blocks = half // BLOCK
    for kind, ref in enumerate((k_ref, v_ref)):
        for which in range(2):
            side = core if which == 0 else 1 - core
            pieces = []
            for i in range(blocks):
                b = side * blocks + i
                scale = table_ref[kind, index_ref[b, head]]
                codes = ref[0, pl.ds(pl.multiple_of(b * BLOCK, BLOCK), BLOCK), :]
                pieces.append((codes.astype(jnp.float32) * scale).astype(jnp.bfloat16))
            whole = jnp.concatenate(pieces, axis=0)
            for j in range(CHUNKS):
                piece = whole[j * part : (j + 1) * part]
                if which == 0:
                    keeps[j][0, kind] = piece
                else:
                    sends[j, 0, kind] = piece


def prepare(core, index, table, key_codes, value_codes):
    tokens = key_codes.shape[1]
    part = tokens // 2 // CHUNKS
    smem = pl.BlockSpec(memory_space=pltpu.SMEM)
    codes = pl.BlockSpec((1, tokens, HD), lambda k: (0, 0, k))
    return pl.pallas_call(
        prepare_kernel,
        grid=(KVH,),
        in_specs=[smem, smem, smem, codes, codes],
        out_specs=[pl.BlockSpec((1, 2, part, HD), lambda k: (k, 0, 0, 0))] * CHUNKS
        + [pl.BlockSpec((CHUNKS, 1, 2, part, HD), lambda k: (0, k, 0, 0, 0))],
        out_shape=[jax.ShapeDtypeStruct((KVH, 2, part, HD), jnp.bfloat16)] * CHUNKS
        + [jax.ShapeDtypeStruct((CHUNKS, KVH, 2, part, HD), jnp.bfloat16)],
        cost_estimate=pl.CostEstimate(flops=0, bytes_accessed=6 * MIB, transcendentals=0),
    )(core, index, table, key_codes, value_codes)


def attend_kernel(first, last, *refs):
    refs = list(refs)
    q_ref, pair = refs[0], refs[1:3]
    refs = refs[3:]
    if not first:
        acc_in, max_in = refs[:2]
        refs = refs[2:]
    if last:
        out_ref = refs[0]
        refs = refs[1:]
    else:
        acc_out, max_out = refs[:2]
        refs = refs[2:]
    sa, sb, ma, mb = refs
    total = q_ref.shape[0]
    tiles = total // TQ
    sources, _, part, _ = pair[0].shape
    span = sources * part

    def finish(tile, acc, top):
        rows = pl.ds(pl.multiple_of(tile * TQ, TQ), TQ)
        if not first:
            before = max_in[rows, :]
            both = jnp.maximum(before, top)
            old, new = jnp.exp2(before - both), jnp.exp2(top - both)
            acc_old = acc_in[rows, :]
            acc = jnp.concatenate(
                [
                    acc[:, :HD] * new + acc_old[:, :HD] * old,
                    acc[:, HD:] * new + acc_old[:, HD:] * old,
                ],
                axis=1,
            )
            top = both
        if not last:
            acc_out[rows, :] = acc
            max_out[rows, :] = top
            return
        sums = acc[:, HD:]
        out = (acc[:, :HD] / sums).astype(jnp.bfloat16)
        lse = (top + jnp.log2(sums)) * LN2
        high = lse.astype(jnp.bfloat16)
        rest = lse - high.astype(jnp.float32)
        middle = rest.astype(jnp.bfloat16)
        low = rest - middle.astype(jnp.float32)
        lane = lax.broadcasted_iota(jnp.int32, (TQ, HD), 1)
        row = lax.broadcasted_iota(jnp.int32, (TQ, HD), 0)
        place = lane - HD // 4 * (row % 4)
        spread = jnp.where(
            place == 0,
            high.astype(jnp.float32),
            jnp.where(place == 1, middle.astype(jnp.float32), jnp.where(place == 2, low, 0.0)),
        ).astype(jnp.bfloat16)
        packed = TQ // 4
        fold = (
            lax.broadcasted_iota(jnp.int32, (packed, TQ), 1) // 4
            == lax.broadcasted_iota(jnp.int32, (packed, TQ), 0)
        ).astype(jnp.bfloat16)
        extra = jnp.dot(fold, spread, preferred_element_type=jnp.float32).astype(jnp.bfloat16)
        slots = TQ // QROWS
        out_ref[pl.ds(tile * slots, slots)] = jnp.concatenate(
            [out.reshape(slots, QROWS, HD), extra.reshape(slots, EXTRA, HD)], axis=1
        )

    def stage(score, weigh, i, s1, m1, s2, m2):
        if weigh:
            top = jnp.broadcast_to(jnp.max(m2[...], axis=1, keepdims=True) * SCALE2, (TQ, HD))
            m2[...] = top
            acc = jnp.zeros((TQ, 2 * HD), jnp.float32)
        if score:
            q = q_ref[pl.ds(pl.multiple_of(i * TQ, TQ), TQ), :]
            best = None
        for side in range(2):
            if score:
                keys = pair[side][:, 0].reshape(span, HD)
                s = lax.dot_general(q, keys, NT, preferred_element_type=jnp.float32)
                s1[:, pl.ds(side * span, span)] = s
                for n in range(span // HD):
                    piece = s[:, n * HD : (n + 1) * HD]
                    best = piece if best is None else jnp.maximum(best, piece)
            if weigh:
                weights = [
                    jnp.exp2(s2[:, pl.ds(side * span + n * HD, HD)] * SCALE2 - m2[...]).astype(
                        jnp.bfloat16
                    )
                    for n in range(span // HD)
                ]
                values = jnp.concatenate(
                    [pair[side][:, 1].reshape(span, HD), jnp.ones((span, HD), jnp.bfloat16)], axis=1
                )
                acc = acc + jnp.dot(
                    jnp.concatenate(weights, axis=1), values, preferred_element_type=jnp.float32
                )
        if score:
            m1[...] = best
        if weigh:
            finish(i - 1, acc, m2[...])

    stage(True, False, 0, sa, ma, sb, mb)

    def double(g, carry):
        stage(True, True, 2 * g + 1, sb, mb, sa, ma)
        stage(True, True, 2 * g + 2, sa, ma, sb, mb)
        return carry

    lax.fori_loop(0, tiles // 2 - 1, double, 0)
    stage(True, True, tiles - 1, sb, mb, sa, ma)
    stage(False, True, tiles, sa, ma, sb, mb)


def attend(first, last, q, own, other, state):
    total = q.shape[0]
    vmem = pl.BlockSpec(memory_space=pltpu.VMEM)
    tokens = 2 * own.shape[0] * own.shape[2]
    if last:
        shapes = jax.ShapeDtypeStruct((total // QROWS, QROWS + EXTRA, HD), jnp.bfloat16)
        outs = vmem
    else:
        shapes = (
            jax.ShapeDtypeStruct((total, 2 * HD), jnp.float32),
            jax.ShapeDtypeStruct((total, HD), jnp.float32),
        )
        outs = (vmem, vmem)
    aliases = {} if first or last else {3: 0, 4: 1}
    return pl.pallas_call(
        functools.partial(attend_kernel, first, last),
        in_specs=[vmem] * (3 + len(state)),
        out_specs=outs,
        out_shape=shapes,
        input_output_aliases=aliases,
        scratch_shapes=[pltpu.VMEM((TQ, tokens), jnp.float32)] * 2
        + [pltpu.VMEM((TQ, HD), jnp.float32)] * 2,
        compiler_params=pltpu.CompilerParams(vmem_limit_bytes=44 * MIB),
        cost_estimate=pl.CostEstimate(
            flops=8 * total * tokens * HD, bytes_accessed=4 * MIB, transcendentals=total * tokens
        ),
    )(q, own, other, *state)


def local_kernel(lens, q_ref, nk_ref, nv_ref, sk_ref, sv_ref, o_ref, l_ref):
    length = lens[pl.program_id(0)]
    heads = arrange(q_ref[0])
    suffix = sk_ref.shape[1]
    new_keys = nk_ref[0].astype(jnp.float32)
    new_values = nv_ref[0].astype(jnp.float32)
    pad = jnp.zeros((GROUP * 2 - STEPS, HD), jnp.float32)
    visible = lax.broadcasted_iota(jnp.int32, (QROWS, suffix), 1) < length
    step = lax.broadcasted_iota(jnp.int32, (QROWS, 2 * GROUP), 0) % STEPS
    fresh = lax.broadcasted_iota(jnp.int32, (QROWS, 2 * GROUP), 1) <= step
    for k in range(KVH):
        lanes = slice(k * HD, (k + 1) * HD)
        q = heads[k].astype(jnp.bfloat16)
        nk = jnp.concatenate([new_keys[:, lanes], pad], axis=0).astype(jnp.bfloat16)
        nv = jnp.concatenate([new_values[:, lanes], pad], axis=0).astype(jnp.bfloat16)
        s = lax.dot_general(q, sk_ref[0, :, lanes], NT, preferred_element_type=jnp.float32)
        n = lax.dot_general(q, nk, NT, preferred_element_type=jnp.float32)
        s = jnp.where(visible, s * SCALE, FLOOR)
        n = jnp.where(fresh, n * SCALE, FLOOR)
        top = jnp.maximum(jnp.max(s, axis=1, keepdims=True), jnp.max(n, axis=1, keepdims=True))
        es, en = jnp.exp(s - top), jnp.exp(n - top)
        sums = jnp.sum(es, axis=1, keepdims=True) + jnp.sum(en, axis=1, keepdims=True)
        out = jnp.dot(
            es.astype(jnp.bfloat16), sv_ref[0, :, lanes], preferred_element_type=jnp.float32
        ) + jnp.dot(en.astype(jnp.bfloat16), nv, preferred_element_type=jnp.float32)
        o_ref[0, k] = out / sums
        l_ref[0, k] = jnp.broadcast_to(top + jnp.log(sums), (QROWS, HD))


def local_attention(lens, queries, new_keys, new_values, suffix_keys, suffix_values):
    rows, suffix, width = suffix_keys.shape

    def by_row(*shape):
        return pl.BlockSpec((1,) + shape, lambda r, lens: (r,) + (0,) * len(shape))

    return pl.pallas_call(
        local_kernel,
        grid_spec=pltpu.PrefetchScalarGridSpec(
            num_scalar_prefetch=1,
            grid=(rows,),
            in_specs=[
                by_row(STEPS, QH * HD),
                by_row(STEPS, width),
                by_row(STEPS, width),
                by_row(suffix, width),
                by_row(suffix, width),
            ],
            out_specs=[by_row(KVH, QROWS, HD)] * 2,
        ),
        out_shape=[jax.ShapeDtypeStruct((rows, KVH, QROWS, HD), jnp.float32)] * 2,
        compiler_params=pltpu.CompilerParams(vmem_limit_bytes=24 * MIB),
        cost_estimate=pl.CostEstimate(
            flops=4 * rows * QH * STEPS * suffix * HD,
            bytes_accessed=10 * MIB,
            transcendentals=rows * QH * STEPS * suffix,
        ),
    )(lens, queries, new_keys, new_values, suffix_keys, suffix_values)


def combine_kernel(names, back_ref, out_ref, lse_ref, o_ref):
    lane = lax.broadcasted_iota(jnp.int32, (QROWS, HD), 1)
    row = lax.broadcasted_iota(jnp.int32, (QROWS, HD), 0)
    mine = lane // (HD // 4) == row % 4
    unfold = (
        lax.broadcasted_iota(jnp.int32, (QROWS, EXTRA), 0) // 4
        == lax.broadcasted_iota(jnp.int32, (QROWS, EXTRA), 1)
    ).astype(jnp.bfloat16)
    for k in range(KVH):
        block = back_ref[0, k]
        prefix_out = block[:QROWS].astype(jnp.float32)
        spread = jnp.dot(unfold, block[QROWS:], preferred_element_type=jnp.float32)
        prefix_lse = jnp.sum(jnp.where(mine, spread, 0.0), axis=1, keepdims=True)
        local_lse = lse_ref[0, k]
        joint = jnp.maximum(local_lse, prefix_lse)
        local_share = jnp.exp(local_lse - joint)
        prefix_share = jnp.exp(prefix_lse - joint)
        mixed = (local_share * out_ref[0, k] + prefix_share * prefix_out) / (
            local_share + prefix_share
        )
        for g in range(GROUP):
            o_ref[0, :, (k * GROUP + g) * HD : (k * GROUP + g + 1) * HD] = mixed[
                g * STEPS : (g + 1) * STEPS
            ].astype(jnp.bfloat16)


def combine(names, back, local_out, local_lse):
    rows = local_out.shape[0]

    def pick(r, names):
        prefix, slot = slot_of_row(names, r, rows)
        return ((prefix // 2) * 4 + slot * 2 + prefix % 2, 0, 0, 0)

    def by_row(*shape):
        return pl.BlockSpec((1,) + shape, lambda r, names: (r,) + (0,) * len(shape))

    return pl.pallas_call(
        combine_kernel,
        grid_spec=pltpu.PrefetchScalarGridSpec(
            num_scalar_prefetch=1,
            grid=(rows,),
            in_specs=[
                pl.BlockSpec((1, KVH, QROWS + EXTRA, HD), pick),
                by_row(KVH, QROWS, HD),
                by_row(KVH, QROWS, HD),
            ],
            out_specs=by_row(STEPS, QH * HD),
        ),
        out_shape=jax.ShapeDtypeStruct((rows, STEPS, QH * HD), jnp.bfloat16),
        cost_estimate=pl.CostEstimate(flops=0, bytes_accessed=4 * MIB, transcendentals=0),
    )(names, back, local_out, local_lse)


def local(
    queries,
    new_keys,
    new_values,
    suffix_keys,
    suffix_values,
    suffix_len,
    row_prefix,
    prefix_key_codes,
    prefix_value_codes,
    scale_index,
    scale_table,
):
    groups = lax.axis_size("prefix")
    shards = lax.axis_size("seq")
    core = lax.axis_index("prefix") % 2
    swap = [(i, i ^ 1) for i in range(groups)]
    names = row_prefix[:, 0]

    *keeps, sends = prepare(
        core.reshape(1).astype(jnp.int32),
        scale_index[0],
        scale_table,
        prefix_key_codes,
        prefix_value_codes,
    )
    outgoing = outgoing_queries(names, queries)
    received = lax.ppermute(sends, "prefix", swap)
    arrived = lax.all_to_all(
        outgoing.reshape(groups * shards, QROWS, HD),
        ("prefix", "seq"),
        split_axis=0,
        concat_axis=0,
        tiled=True,
    )
    q = arrived.reshape(-1, HD)
    pairs = []
    for j in range(CHUNKS):
        first = jnp.where(core == 0, keeps[j], received[j])
        second = jnp.where(core == 0, received[j], keeps[j])
        own = lax.all_to_all(
            jnp.concatenate([first, second], axis=0), "seq", split_axis=0, concat_axis=0, tiled=True
        )
        pairs.append((own, lax.ppermute(own, "prefix", swap)))
    local_out, local_lse = local_attention(
        suffix_len, queries, new_keys, new_values, suffix_keys, suffix_values
    )
    state = ()
    for j in range(CHUNKS):
        state = attend(j == 0, j == CHUNKS - 1, q, *pairs[j], state)
    back = lax.all_to_all(state, ("prefix", "seq"), split_axis=0, concat_axis=0, tiled=True)
    back = back.reshape(groups * SLOTS, KVH, QROWS + EXTRA, HD)
    return combine(names, back, local_out, local_lse)


def solution(mesh):
    return jax.shard_map(
        local,
        mesh=mesh,
        in_specs=(
            P(("prefix", "seq"), None, None),
            P(("prefix", "seq"), None, None),
            P(("prefix", "seq"), None, None),
            P(("prefix", "seq"), None, None),
            P(("prefix", "seq"), None, None),
            P(("prefix", "seq")),
            P(("prefix", "seq"), None),
            P("prefix", "seq", None),
            P("prefix", "seq", None),
            P("prefix", "seq", None),
            P(),
        ),
        out_specs=P(("prefix", "seq"), None, None),
        check_vma=False,
    )
```

```python
import functools
import math

import jax
import jax.numpy as jnp
from jax import lax
from jax.experimental import pallas as pl
from jax.experimental.pallas import tpu as pltpu
from jax.sharding import PartitionSpec as P

QH = 64
KVH = 8
HD = 128
STEPS = 4
BLOCK = 128
GROUP = QH // KVH
QROWS = GROUP * STEPS
SLOTS = 2
PASSES = 2
PIECES = 2
TQ = 256
EXTRA = 8
SCALE = HD**-0.5
SCALE2 = SCALE * math.log2(math.e)
LN2 = math.log(2.0)
FLOOR = -1e30
NT = (((1,), (1,)), ((), ()))
MIB = 2**20


def arrange(rows):
    wide = rows.astype(jnp.float32)
    heads = []
    for k in range(KVH):
        parts = [wide[:, (k * GROUP + g) * HD : (k * GROUP + g + 1) * HD] for g in range(GROUP)]
        heads.append(jnp.concatenate(parts, axis=0))
    return heads


def slot_of_row(names, row, rows):
    prefix = names[row]
    seen = jnp.int32(0)
    for r in range(rows):
        earlier = jnp.logical_and(names[r] == prefix, r < row)
        seen = seen + earlier.astype(jnp.int32)
    return prefix, seen


def slot_index(prefix, slot):
    return (prefix // 2) * (2 * SLOTS) + slot * 2 + prefix % 2


def outgoing_kernel(names, q_ref, o_ref, a_ref):
    rows = q_ref.shape[0]
    o_ref[...] = jnp.zeros_like(o_ref)
    for r in range(rows):
        prefix, slot = slot_of_row(names, r, rows)
        place = slot_index(prefix, slot)
        heads = arrange(q_ref[r])
        for k in range(KVH):
            head = heads[k].astype(jnp.bfloat16)
            o_ref[place, k] = head
            a_ref[r, k] = head


def outgoing_queries(names, queries):
    slots = 8 * SLOTS
    return pl.pallas_call(
        outgoing_kernel,
        in_specs=[
            pl.BlockSpec(memory_space=pltpu.SMEM),
            pl.BlockSpec(memory_space=pltpu.VMEM),
        ],
        out_specs=[pl.BlockSpec(memory_space=pltpu.VMEM)] * 2,
        out_shape=[
            jax.ShapeDtypeStruct((slots, KVH, QROWS, HD), jnp.bfloat16),
            jax.ShapeDtypeStruct((queries.shape[0], KVH, QROWS, HD), jnp.bfloat16),
        ],
        cost_estimate=pl.CostEstimate(flops=0, bytes_accessed=2 * MIB, transcendentals=0),
    )(names, queries)


def prepare_kernel(core_ref, index_ref, table_ref, k_ref, v_ref, keep_ref, send_ref):
    head = pl.program_id(0)
    core = core_ref[0]
    blocks = keep_ref.shape[2] // BLOCK
    for kind, ref in enumerate((k_ref, v_ref)):
        for side, out_ref in ((core, keep_ref), (1 - core, send_ref)):
            for i in range(blocks):
                b = side * blocks + i
                scale = table_ref[kind, index_ref[b, head]]
                codes = ref[0, pl.ds(pl.multiple_of(b * BLOCK, BLOCK), BLOCK), :]
                scaled = codes.astype(jnp.float32) * scale
                if kind == 1:
                    scaled = scaled.T
                out_ref[0, kind, pl.ds(i * BLOCK, BLOCK)] = scaled.astype(jnp.bfloat16)


def prepare(core, index, table, key_codes, value_codes):
    tokens = key_codes.shape[1]
    half = tokens // 2
    smem = pl.BlockSpec(memory_space=pltpu.SMEM)
    codes = pl.BlockSpec((1, tokens, HD), lambda k, core: (0, 0, k))
    block = (1, 2, half, HD)
    return pl.pallas_call(
        prepare_kernel,
        grid_spec=pltpu.PrefetchScalarGridSpec(
            num_scalar_prefetch=1,
            grid=(KVH,),
            in_specs=[smem, smem, codes, codes],
            out_specs=[
                pl.BlockSpec(block, lambda k, core: (core[0] * KVH + k, 0, 0, 0)),
                pl.BlockSpec(block, lambda k, core: (k, 0, 0, 0)),
            ],
        ),
        out_shape=[
            jax.ShapeDtypeStruct((2 * KVH, 2, half, HD), jnp.bfloat16),
            jax.ShapeDtypeStruct((KVH, 2, half, HD), jnp.bfloat16),
        ],
        cost_estimate=pl.CostEstimate(flops=0, bytes_accessed=MIB // 8, transcendentals=0),
    )(core, index, table, key_codes, value_codes)


def attend_kernel(first, last, *refs):
    refs = list(refs)
    q_ref, kv_ref = refs[:2]
    refs = refs[2:]
    before_ref = None if first else refs.pop(0)
    if last:
        out_ref = refs.pop(0)
        sa, sb, ma, mb, mid_ref = refs
    else:
        mid_ref, sa, sb, ma, mb = refs
    total = q_ref.shape[0]
    tiles = total // TQ
    sources, _, part, _ = kv_ref.shape
    run = sources // PASSES
    span = run * part

    def finish(turn, tile, both, top):
        columns = pl.ds(pl.multiple_of(tile * TQ, TQ), TQ)
        acc, sums = both[:HD], both[HD : HD + 8]
        if turn > 0 or not first:
            old_ref = mid_ref if turn > 0 else before_ref
            old_top = old_ref[HD + 8 :, columns]
            joint = jnp.maximum(old_top, top)
            old, new = jnp.exp2(old_top - joint), jnp.exp2(top - joint)
            acc = acc * new[:1] + old_ref[:HD, columns] * old[:1]
            sums = sums * new + old_ref[HD : HD + 8, columns] * old
            top = joint
        if turn < PASSES - 1 or not last:
            mid_ref[:HD, columns] = acc
            mid_ref[HD : HD + 8, columns] = sums
            mid_ref[HD + 8 :, columns] = top
            return
        out = (acc * (1.0 / sums[:1])).T.astype(jnp.bfloat16)
        lse = (top + jnp.log2(sums)) * LN2
        high = lse.astype(jnp.bfloat16).astype(jnp.float32)
        middle = (lse - high).astype(jnp.bfloat16).astype(jnp.float32)
        low = lse - high - middle
        line = lax.broadcasted_iota(jnp.int32, (EXTRA, TQ), 0)
        parts = jnp.where(line == 0, high, jnp.where(line == 1, middle, low)).astype(jnp.bfloat16)
        slots = TQ // QROWS
        out_ref[pl.ds(tile * slots, slots), :QROWS] = out.reshape(slots, QROWS, HD)
        for n in range(slots):
            lanes = n * QROWS // HD * HD
            out_ref[tile * slots + n, QROWS:] = parts[:, lanes : lanes + HD]

    def stage(score, weigh, s1, m1, s2, m2):
        if weigh:
            top = jnp.broadcast_to(jnp.max(m2[...], axis=0, keepdims=True) * SCALE2, (8, TQ))
        if score:
            q = q_ref[pl.ds(pl.multiple_of(score[1] * TQ, TQ), TQ), :]
            best = None
        both = None
        step = run // PIECES
        piece = step * part
        for n in range(PIECES):
            tokens = pl.ds(n * piece, piece)
            if score:
                keys = kv_ref[pl.ds(score[0] * run + n * step, step), 0].reshape(piece, HD)
                s = lax.dot_general(keys, q, NT, preferred_element_type=jnp.float32)
                s1[tokens, :] = s
                high = jnp.max(s.reshape(piece // 8, 8, TQ), axis=0)
                best = high if best is None else jnp.maximum(best, high)
            if weigh:
                weights = jnp.exp2(s2[tokens, :] * SCALE2 - top[:1]).astype(jnp.bfloat16)
                values = [
                    kv_ref[weigh[0] * run + n * step + j, 1, pl.ds(i * BLOCK, BLOCK), :]
                    for j in range(step)
                    for i in range(part // BLOCK)
                ]
                values = jnp.concatenate(values, axis=1)
                values = jnp.concatenate([values, jnp.ones((16, piece), jnp.bfloat16)], axis=0)
                more = jnp.dot(values, weights, preferred_element_type=jnp.float32)
                both = more if both is None else both + more
        if score:
            m1[...] = best
        if weigh:
            finish(weigh[0], weigh[1], both, top)

    stage((0, 0), None, sa, ma, sb, mb)
    for turn in range(PASSES):

        def double(g, carry):
            stage((turn, 2 * g + 1), (turn, 2 * g), sb, mb, sa, ma)
            stage((turn, 2 * g + 2), (turn, 2 * g + 1), sa, ma, sb, mb)
            return carry

        lax.fori_loop(0, tiles // 2 - 1, double, 0)
        stage((turn, tiles - 1), (turn, tiles - 2), sb, mb, sa, ma)
        following = (turn + 1, 0) if turn + 1 < PASSES else None
        stage(following, (turn, tiles - 1), sa, ma, sb, mb)


def attend(first, last, q, kv, state):
    total = q.shape[0]
    vmem = pl.BlockSpec(memory_space=pltpu.VMEM)
    tokens = kv.shape[0] * kv.shape[2]
    scratch = [pltpu.VMEM((tokens // PASSES, TQ), jnp.float32)] * 2
    scratch += [pltpu.VMEM((8, TQ), jnp.float32)] * 2
    held = (HD + 16, total)
    if last:
        shape = jax.ShapeDtypeStruct((total // QROWS, QROWS + EXTRA, HD), jnp.bfloat16)
        scratch.append(pltpu.VMEM(held, jnp.float32))
    else:
        shape = jax.ShapeDtypeStruct(held, jnp.float32)
    return pl.pallas_call(
        functools.partial(attend_kernel, first, last),
        in_specs=[vmem] * (2 + len(state)),
        out_specs=vmem,
        out_shape=shape,
        scratch_shapes=scratch,
        compiler_params=pltpu.CompilerParams(vmem_limit_bytes=40 * MIB),
        cost_estimate=pl.CostEstimate(
            flops=8 * total * tokens * HD, bytes_accessed=4 * MIB, transcendentals=total * tokens
        ),
    )(q, kv, *state)


def local_kernel(lens, q_ref, nk_ref, nv_ref, sk_ref, sv_ref, o_ref, l_ref):
    length = lens[pl.program_id(0)]
    suffix = sk_ref.shape[1]
    new_keys = nk_ref[0].astype(jnp.float32)
    new_values = nv_ref[0].astype(jnp.float32)
    pad = jnp.zeros((GROUP * 2 - STEPS, HD), jnp.float32)
    visible = lax.broadcasted_iota(jnp.int32, (QROWS, suffix), 1) < length
    step = lax.broadcasted_iota(jnp.int32, (QROWS, 2 * GROUP), 0) % STEPS
    fresh = lax.broadcasted_iota(jnp.int32, (QROWS, 2 * GROUP), 1) <= step
    for k in range(KVH):
        lanes = slice(k * HD, (k + 1) * HD)
        q = q_ref[0, k]
        nk = jnp.concatenate([new_keys[:, lanes], pad], axis=0).astype(jnp.bfloat16)
        nv = jnp.concatenate([new_values[:, lanes], pad], axis=0).astype(jnp.bfloat16)
        s = lax.dot_general(q, sk_ref[0, :, lanes], NT, preferred_element_type=jnp.float32)
        n = lax.dot_general(q, nk, NT, preferred_element_type=jnp.float32)
        s = jnp.where(visible, s * SCALE, FLOOR)
        n = jnp.where(fresh, n * SCALE, FLOOR)
        top = jnp.maximum(jnp.max(s, axis=1, keepdims=True), jnp.max(n, axis=1, keepdims=True))
        es, en = jnp.exp(s - top), jnp.exp(n - top)
        sums = jnp.sum(es, axis=1, keepdims=True) + jnp.sum(en, axis=1, keepdims=True)
        out = jnp.dot(
            es.astype(jnp.bfloat16), sv_ref[0, :, lanes], preferred_element_type=jnp.float32
        ) + jnp.dot(en.astype(jnp.bfloat16), nv, preferred_element_type=jnp.float32)
        o_ref[0, k] = out / sums
        l_ref[0, k] = jnp.broadcast_to(top + jnp.log(sums), (QROWS, HD))


def local_attention(lens, queries, new_keys, new_values, suffix_keys, suffix_values):
    rows, suffix, width = suffix_keys.shape

    def by_row(*shape):
        return pl.BlockSpec((1,) + shape, lambda r, lens: (r,) + (0,) * len(shape))

    return pl.pallas_call(
        local_kernel,
        grid_spec=pltpu.PrefetchScalarGridSpec(
            num_scalar_prefetch=1,
            grid=(rows,),
            in_specs=[
                by_row(KVH, QROWS, HD),
                by_row(STEPS, width),
                by_row(STEPS, width),
                by_row(suffix, width),
                by_row(suffix, width),
            ],
            out_specs=[by_row(KVH, QROWS, HD)] * 2,
        ),
        out_shape=[jax.ShapeDtypeStruct((rows, KVH, QROWS, HD), jnp.float32)] * 2,
        compiler_params=pltpu.CompilerParams(vmem_limit_bytes=24 * MIB),
        cost_estimate=pl.CostEstimate(
            flops=4 * rows * QH * STEPS * suffix * HD,
            bytes_accessed=10 * MIB,
            transcendentals=rows * QH * STEPS * suffix,
        ),
    )(lens, queries, new_keys, new_values, in_hbm(suffix_keys), in_hbm(suffix_values))


def combine_kernel(names, first_lane, back_ref, out_ref, lse_ref, o_ref):
    rows = out_ref.shape[0]
    lane = lax.broadcasted_iota(jnp.int32, (QROWS, HD), 1)
    row = lax.broadcasted_iota(jnp.int32, (QROWS, HD), 0)
    mine = lane == row + first_lane[0]

    def mix(r, carry):
        prefix, slot = slot_of_row(names, r, rows)
        place = slot_index(prefix, slot)
        for k in range(KVH):
            prefix_out = back_ref[place, k, :QROWS].astype(jnp.float32)
            parts = back_ref[place, k, QROWS:].astype(jnp.float32)
            spread = jnp.where(mine, parts[:1] + parts[1:2] + parts[2:3], 0.0)
            prefix_lse = jnp.sum(spread, axis=1, keepdims=True)
            local_lse = lse_ref[r, k]
            joint = jnp.maximum(local_lse, prefix_lse)
            local_share = jnp.exp(local_lse - joint)
            prefix_share = jnp.exp(prefix_lse - joint)
            mixed = (local_share * out_ref[r, k] + prefix_share * prefix_out) / (
                local_share + prefix_share
            )
            for g in range(GROUP):
                o_ref[r, :, (k * GROUP + g) * HD : (k * GROUP + g + 1) * HD] = mixed[
                    g * STEPS : (g + 1) * STEPS
                ].astype(jnp.bfloat16)
        return carry

    lax.fori_loop(0, rows, mix, 0)


def in_hbm(x):
    return pltpu.with_memory_space_constraint(x, pltpu.HBM)


def combine(names, first_lane, back, local_out, local_lse):
    rows = local_out.shape[0]
    vmem = pl.BlockSpec(memory_space=pltpu.VMEM)
    return pl.pallas_call(
        combine_kernel,
        in_specs=[pl.BlockSpec(memory_space=pltpu.SMEM)] * 2 + [vmem] * 3,
        out_specs=vmem,
        out_shape=jax.ShapeDtypeStruct((rows, STEPS, QH * HD), jnp.bfloat16),
        cost_estimate=pl.CostEstimate(flops=0, bytes_accessed=4 * MIB, transcendentals=0),
    )(names, first_lane, in_hbm(back), in_hbm(local_out), in_hbm(local_lse))


def local(
    queries,
    new_keys,
    new_values,
    suffix_keys,
    suffix_values,
    suffix_len,
    row_prefix,
    prefix_key_codes,
    prefix_value_codes,
    scale_index,
    scale_table,
):
    groups = lax.axis_size("prefix")
    shards = lax.axis_size("seq")
    core = lax.axis_index("prefix") % 2
    swap = [(i, i ^ 1) for i in range(groups)]
    names = row_prefix[:, 0]

    outgoing, arranged = outgoing_queries(names, queries)
    outgoing, key_codes, value_codes = lax.optimization_barrier(
        (outgoing, prefix_key_codes, prefix_value_codes)
    )
    arrived = lax.all_to_all(
        outgoing.reshape(groups * shards, QROWS, HD),
        ("prefix", "seq"),
        split_axis=0,
        concat_axis=0,
        tiled=True,
    )
    keep, send = prepare(
        core.reshape(1).astype(jnp.int32), scale_index[0], scale_table, key_codes, value_codes
    )
    received = lax.ppermute(send, "prefix", swap)
    q = arrived.reshape(-1, HD)
    moved = lax.dynamic_update_slice(keep, received, ((1 - core) * KVH, 0, 0, 0))
    moved, q = lax.optimization_barrier((moved, q))
    own = lax.all_to_all(moved, "seq", split_axis=0, concat_axis=0, tiled=True)
    other = lax.ppermute(own, "prefix", swap)
    state = attend(True, False, q, own, ())
    answer = attend(False, True, q, other, (state,))
    local_out, local_lse = local_attention(
        suffix_len, arranged, new_keys, new_values, suffix_keys, suffix_values
    )
    back = lax.all_to_all(answer, ("prefix", "seq"), split_axis=0, concat_axis=0, tiled=True)
    back = back.reshape(groups * SLOTS, KVH, QROWS + EXTRA, HD)
    first_lane = lax.axis_index("seq") % (HD // QROWS) * QROWS
    return combine(names, first_lane.reshape(1).astype(jnp.int32), back, local_out, local_lse)


def solution(mesh):
    return jax.shard_map(
        local,
        mesh=mesh,
        in_specs=(
            P(("prefix", "seq"), None, None),
            P(("prefix", "seq"), None, None),
            P(("prefix", "seq"), None, None),
            P(("prefix", "seq"), None, None),
            P(("prefix", "seq"), None, None),
            P(("prefix", "seq")),
            P(("prefix", "seq"), None),
            P("prefix", "seq", None),
            P("prefix", "seq", None),
            P("prefix", "seq", None),
            P(),
        ),
        out_specs=P(("prefix", "seq"), None, None),
        check_vma=False,
    )
```

```python
import functools
import math

import jax
import jax.numpy as jnp
from jax import lax
from jax.experimental import pallas as pl
from jax.experimental.pallas import tpu as pltpu
from jax.sharding import PartitionSpec as P

QH = 64
KVH = 8
HD = 128
STEPS = 4
BLOCK = 128
GROUP = QH // KVH
QROWS = GROUP * STEPS
SLOTS = 2
PASSES = 2
PIECES = 2
TQ = 256
EXTRA = 8
SCALE = HD**-0.5
SCALE2 = SCALE * math.log2(math.e)
LN2 = math.log(2.0)
FLOOR = -1e30
NT = (((1,), (1,)), ((), ()))
MIB = 2**20


def arrange(rows):
    wide = rows.astype(jnp.float32)
    heads = []
    for k in range(KVH):
        parts = [wide[:, (k * GROUP + g) * HD : (k * GROUP + g + 1) * HD] for g in range(GROUP)]
        heads.append(jnp.concatenate(parts, axis=0))
    return heads


def slot_of_row(names, row, rows):
    prefix = names[row]
    seen = jnp.int32(0)
    for r in range(rows):
        earlier = jnp.logical_and(names[r] == prefix, r < row)
        seen = seen + earlier.astype(jnp.int32)
    return prefix, seen


def slot_index(prefix, slot):
    return (prefix // 2) * (2 * SLOTS) + slot * 2 + prefix % 2


def outgoing_kernel(names, q_ref, o_ref, a_ref):
    rows = q_ref.shape[0]
    o_ref[...] = jnp.zeros_like(o_ref)
    for r in range(rows):
        prefix, slot = slot_of_row(names, r, rows)
        place = slot_index(prefix, slot)
        heads = arrange(q_ref[r])
        for k in range(KVH):
            head = heads[k].astype(jnp.bfloat16)
            o_ref[place, k] = head
            a_ref[r, k] = head


def outgoing_queries(names, queries):
    slots = 8 * SLOTS
    return pl.pallas_call(
        outgoing_kernel,
        in_specs=[
            pl.BlockSpec(memory_space=pltpu.SMEM),
            pl.BlockSpec(memory_space=pltpu.VMEM),
        ],
        out_specs=[pl.BlockSpec(memory_space=pltpu.VMEM)] * 2,
        out_shape=[
            jax.ShapeDtypeStruct((slots, KVH, QROWS, HD), jnp.bfloat16),
            jax.ShapeDtypeStruct((queries.shape[0], KVH, QROWS, HD), jnp.bfloat16),
        ],
        cost_estimate=pl.CostEstimate(flops=0, bytes_accessed=2 * MIB, transcendentals=0),
    )(names, queries)


def prepare_kernel(core_ref, mine_ref, other_ref, table_ref, k_ref, v_ref, got_ref, o_ref):
    head = pl.program_id(0)
    core = core_ref[0]
    blocks = o_ref.shape[3] // BLOCK
    for source in range(2):
        place = core if source == 0 else 1 - core
        index_ref = mine_ref if source == 0 else other_ref
        for kind in range(2):
            for i in range(blocks):
                tokens = pl.ds(i * BLOCK, BLOCK)
                scale = table_ref[kind, index_ref[core * blocks + i, head]]
                if source == 0:
                    codes = (k_ref, v_ref)[kind][0, tokens, :]
                else:
                    codes = got_ref[kind, tokens, :]
                scaled = codes.astype(jnp.float32) * scale
                if kind == 1:
                    scaled = scaled.T
                o_ref[place, 0, kind, tokens] = scaled.astype(jnp.bfloat16)


def prepare(core, index, other_index, table, key_codes, value_codes, received):
    half = key_codes.shape[1] // 2
    smem = pl.BlockSpec(memory_space=pltpu.SMEM)
    codes = pl.BlockSpec((1, half, HD), lambda k, core: (0, core[0], k))
    return pl.pallas_call(
        prepare_kernel,
        grid_spec=pltpu.PrefetchScalarGridSpec(
            num_scalar_prefetch=1,
            grid=(KVH,),
            in_specs=[smem] * 3
            + [codes, codes, pl.BlockSpec((2, half, HD), lambda k, core: (0, 0, k))],
            out_specs=pl.BlockSpec((2, 1, 2, half, HD), lambda k, core: (0, k, 0, 0, 0)),
        ),
        out_shape=jax.ShapeDtypeStruct((2, KVH, 2, half, HD), jnp.bfloat16),
        cost_estimate=pl.CostEstimate(flops=0, bytes_accessed=12 * MIB, transcendentals=0),
    )(core, index, other_index, table, key_codes, value_codes, received)


def attend_kernel(first, last, *refs):
    refs = list(refs)
    q_ref, kv_ref = refs[:2]
    refs = refs[2:]
    before_ref = None if first else refs.pop(0)
    if last:
        out_ref = refs.pop(0)
        sa, sb, ma, mb, mid_ref = refs
    else:
        mid_ref, sa, sb, ma, mb = refs
    total = q_ref.shape[0]
    tiles = total // TQ
    sources, _, part, _ = kv_ref.shape
    run = sources // PASSES
    span = run * part

    def finish(turn, tile, both, top):
        columns = pl.ds(pl.multiple_of(tile * TQ, TQ), TQ)
        acc, sums = both[:HD], both[HD : HD + 8]
        if turn > 0 or not first:
            old_ref = mid_ref if turn > 0 else before_ref
            old_top = old_ref[HD + 8 :, columns]
            joint = jnp.maximum(old_top, top)
            old, new = jnp.exp2(old_top - joint), jnp.exp2(top - joint)
            acc = acc * new[:1] + old_ref[:HD, columns] * old[:1]
            sums = sums * new + old_ref[HD : HD + 8, columns] * old
            top = joint
        if turn < PASSES - 1 or not last:
            mid_ref[:HD, columns] = acc
            mid_ref[HD : HD + 8, columns] = sums
            mid_ref[HD + 8 :, columns] = top
            return
        out = (acc * (1.0 / sums[:1])).T.astype(jnp.bfloat16)
        lse = (top + jnp.log2(sums)) * LN2
        high = lse.astype(jnp.bfloat16).astype(jnp.float32)
        middle = (lse - high).astype(jnp.bfloat16).astype(jnp.float32)
        low = lse - high - middle
        line = lax.broadcasted_iota(jnp.int32, (EXTRA, TQ), 0)
        parts = jnp.where(line == 0, high, jnp.where(line == 1, middle, low)).astype(jnp.bfloat16)
        slots = TQ // QROWS
        out_ref[pl.ds(tile * slots, slots), :QROWS] = out.reshape(slots, QROWS, HD)
        for n in range(slots):
            lanes = n * QROWS // HD * HD
            out_ref[tile * slots + n, QROWS:] = parts[:, lanes : lanes + HD]

    def stage(score, weigh, s1, m1, s2, m2):
        if weigh:
            top = jnp.broadcast_to(jnp.max(m2[...], axis=0, keepdims=True) * SCALE2, (8, TQ))
        if score:
            q = q_ref[pl.ds(pl.multiple_of(score[1] * TQ, TQ), TQ), :]
            best = None
        both = None
        step = run // PIECES
        piece = step * part
        for n in range(PIECES):
            tokens = pl.ds(n * piece, piece)
            if score:
                keys = kv_ref[pl.ds(score[0] * run + n * step, step), 0].reshape(piece, HD)
                s = lax.dot_general(keys, q, NT, preferred_element_type=jnp.float32)
                s1[tokens, :] = s
                high = jnp.max(s.reshape(piece // 8, 8, TQ), axis=0)
                best = high if best is None else jnp.maximum(best, high)
            if weigh:
                weights = jnp.exp2(s2[tokens, :] * SCALE2 - top[:1]).astype(jnp.bfloat16)
                values = [
                    kv_ref[weigh[0] * run + n * step + j, 1, pl.ds(i * BLOCK, BLOCK), :]
                    for j in range(step)
                    for i in range(part // BLOCK)
                ]
                values = jnp.concatenate(values, axis=1)
                values = jnp.concatenate([values, jnp.ones((16, piece), jnp.bfloat16)], axis=0)
                more = jnp.dot(values, weights, preferred_element_type=jnp.float32)
                both = more if both is None else both + more
        if score:
            m1[...] = best
        if weigh:
            finish(weigh[0], weigh[1], both, top)

    stage((0, 0), None, sa, ma, sb, mb)
    for turn in range(PASSES):

        def double(g, carry):
            stage((turn, 2 * g + 1), (turn, 2 * g), sb, mb, sa, ma)
            stage((turn, 2 * g + 2), (turn, 2 * g + 1), sa, ma, sb, mb)
            return carry

        lax.fori_loop(0, tiles // 2 - 1, double, 0)
        stage((turn, tiles - 1), (turn, tiles - 2), sb, mb, sa, ma)
        following = (turn + 1, 0) if turn + 1 < PASSES else None
        stage(following, (turn, tiles - 1), sa, ma, sb, mb)


def attend(first, last, q, kv, state):
    total = q.shape[0]
    vmem = pl.BlockSpec(memory_space=pltpu.VMEM)
    tokens = kv.shape[0] * kv.shape[2]
    scratch = [pltpu.VMEM((tokens // PASSES, TQ), jnp.float32)] * 2
    scratch += [pltpu.VMEM((8, TQ), jnp.float32)] * 2
    held = (HD + 16, total)
    if last:
        shape = jax.ShapeDtypeStruct((total // QROWS, QROWS + EXTRA, HD), jnp.bfloat16)
        scratch.append(pltpu.VMEM(held, jnp.float32))
    else:
        shape = jax.ShapeDtypeStruct(held, jnp.float32)
    return pl.pallas_call(
        functools.partial(attend_kernel, first, last),
        in_specs=[vmem] * (2 + len(state)),
        out_specs=vmem,
        out_shape=shape,
        scratch_shapes=scratch,
        compiler_params=pltpu.CompilerParams(vmem_limit_bytes=40 * MIB),
        cost_estimate=pl.CostEstimate(
            flops=8 * total * tokens * HD, bytes_accessed=4 * MIB, transcendentals=total * tokens
        ),
    )(q, kv, *state)


def local_kernel(lens, q_ref, nk_ref, nv_ref, sk_ref, sv_ref, o_ref, l_ref):
    length = lens[pl.program_id(0)]
    suffix = sk_ref.shape[1]
    new_keys = nk_ref[0].astype(jnp.float32)
    new_values = nv_ref[0].astype(jnp.float32)
    pad = jnp.zeros((GROUP * 2 - STEPS, HD), jnp.float32)
    visible = lax.broadcasted_iota(jnp.int32, (QROWS, suffix), 1) < length
    step = lax.broadcasted_iota(jnp.int32, (QROWS, 2 * GROUP), 0) % STEPS
    fresh = lax.broadcasted_iota(jnp.int32, (QROWS, 2 * GROUP), 1) <= step
    for k in range(KVH):
        lanes = slice(k * HD, (k + 1) * HD)
        q = q_ref[0, k]
        nk = jnp.concatenate([new_keys[:, lanes], pad], axis=0).astype(jnp.bfloat16)
        nv = jnp.concatenate([new_values[:, lanes], pad], axis=0).astype(jnp.bfloat16)
        s = lax.dot_general(q, sk_ref[0, :, lanes], NT, preferred_element_type=jnp.float32)
        n = lax.dot_general(q, nk, NT, preferred_element_type=jnp.float32)
        s = jnp.where(visible, s * SCALE, FLOOR)
        n = jnp.where(fresh, n * SCALE, FLOOR)
        top = jnp.maximum(jnp.max(s, axis=1, keepdims=True), jnp.max(n, axis=1, keepdims=True))
        es, en = jnp.exp(s - top), jnp.exp(n - top)
        sums = jnp.sum(es, axis=1, keepdims=True) + jnp.sum(en, axis=1, keepdims=True)
        out = jnp.dot(
            es.astype(jnp.bfloat16), sv_ref[0, :, lanes], preferred_element_type=jnp.float32
        ) + jnp.dot(en.astype(jnp.bfloat16), nv, preferred_element_type=jnp.float32)
        o_ref[0, k] = out / sums
        l_ref[0, k] = jnp.broadcast_to(top + jnp.log(sums), (QROWS, HD))


def local_attention(lens, queries, new_keys, new_values, suffix_keys, suffix_values):
    rows, suffix, width = suffix_keys.shape

    def by_row(*shape):
        return pl.BlockSpec((1,) + shape, lambda r, lens: (r,) + (0,) * len(shape))

    return pl.pallas_call(
        local_kernel,
        grid_spec=pltpu.PrefetchScalarGridSpec(
            num_scalar_prefetch=1,
            grid=(rows,),
            in_specs=[
                by_row(KVH, QROWS, HD),
                by_row(STEPS, width),
                by_row(STEPS, width),
                by_row(suffix, width),
                by_row(suffix, width),
            ],
            out_specs=[by_row(KVH, QROWS, HD)] * 2,
        ),
        out_shape=[pltpu.HBM((rows, KVH, QROWS, HD), jnp.float32)] * 2,
        compiler_params=pltpu.CompilerParams(vmem_limit_bytes=24 * MIB),
        cost_estimate=pl.CostEstimate(
            flops=4 * rows * QH * STEPS * suffix * HD,
            bytes_accessed=10 * MIB,
            transcendentals=rows * QH * STEPS * suffix,
        ),
    )(lens, queries, new_keys, new_values, in_hbm(suffix_keys), in_hbm(suffix_values))


def combine_kernel(names, first_lane, back_ref, out_ref, lse_ref, o_ref):
    rows = out_ref.shape[0]
    lane = lax.broadcasted_iota(jnp.int32, (QROWS, HD), 1)
    row = lax.broadcasted_iota(jnp.int32, (QROWS, HD), 0)
    mine = lane == row + first_lane[0]

    def mix(r, carry):
        prefix, slot = slot_of_row(names, r, rows)
        place = slot_index(prefix, slot)
        for k in range(KVH):
            prefix_out = back_ref[place, k, :QROWS].astype(jnp.float32)
            parts = back_ref[place, k, QROWS:].astype(jnp.float32)
            spread = jnp.where(mine, parts[:1] + parts[1:2] + parts[2:3], 0.0)
            prefix_lse = jnp.sum(spread, axis=1, keepdims=True)
            local_lse = lse_ref[r, k]
            joint = jnp.maximum(local_lse, prefix_lse)
            local_share = jnp.exp(local_lse - joint)
            prefix_share = jnp.exp(prefix_lse - joint)
            mixed = (local_share * out_ref[r, k] + prefix_share * prefix_out) / (
                local_share + prefix_share
            )
            for g in range(GROUP):
                o_ref[r, :, (k * GROUP + g) * HD : (k * GROUP + g + 1) * HD] = mixed[
                    g * STEPS : (g + 1) * STEPS
                ].astype(jnp.bfloat16)
        return carry

    lax.fori_loop(0, rows, mix, 0)


def in_hbm(x):
    return pltpu.with_memory_space_constraint(x, pltpu.HBM)


def combine(names, first_lane, back, local_out, local_lse):
    rows = local_out.shape[0]
    vmem = pl.BlockSpec(memory_space=pltpu.VMEM)
    return pl.pallas_call(
        combine_kernel,
        in_specs=[pl.BlockSpec(memory_space=pltpu.SMEM)] * 2 + [vmem] * 3,
        out_specs=vmem,
        out_shape=jax.ShapeDtypeStruct((rows, STEPS, QH * HD), jnp.bfloat16),
        cost_estimate=pl.CostEstimate(flops=0, bytes_accessed=4 * MIB, transcendentals=0),
    )(names, first_lane, in_hbm(back), in_hbm(local_out), in_hbm(local_lse))


def local(
    queries,
    new_keys,
    new_values,
    suffix_keys,
    suffix_values,
    suffix_len,
    row_prefix,
    prefix_key_codes,
    prefix_value_codes,
    scale_index,
    scale_table,
):
    groups = lax.axis_size("prefix")
    shards = lax.axis_size("seq")
    core = lax.axis_index("prefix") % 2
    swap = [(i, i ^ 1) for i in range(groups)]
    names = row_prefix[:, 0]

    half = prefix_key_codes.shape[1] // 2
    sent = [
        lax.dynamic_slice_in_dim(codes[0], (1 - core) * half, half, 0)
        for codes in (prefix_key_codes, prefix_value_codes)
    ]
    received = lax.ppermute(jnp.stack(sent), "prefix", swap)
    other_index = lax.ppermute(scale_index, "prefix", swap)
    outgoing, arranged = outgoing_queries(names, queries)
    arrived = lax.all_to_all(
        outgoing.reshape(groups * shards, QROWS, HD),
        ("prefix", "seq"),
        split_axis=0,
        concat_axis=0,
        tiled=True,
    )
    q = arrived.reshape(-1, HD)
    moved = prepare(
        core.reshape(1).astype(jnp.int32),
        scale_index[0],
        other_index[0],
        scale_table,
        prefix_key_codes,
        prefix_value_codes,
        received,
    ).reshape(2 * KVH, 2, half, HD)
    moved, q = lax.optimization_barrier((moved, q))
    own = lax.all_to_all(moved, "seq", split_axis=0, concat_axis=0, tiled=True)
    other = lax.ppermute(own, "prefix", swap)
    state = attend(True, False, q, own, ())
    answer = attend(False, True, q, other, (state,))
    local_out, local_lse = local_attention(
        suffix_len, arranged, new_keys, new_values, suffix_keys, suffix_values
    )
    back = lax.all_to_all(answer, ("prefix", "seq"), split_axis=0, concat_axis=0, tiled=True)
    back = back.reshape(groups * SLOTS, KVH, QROWS + EXTRA, HD)
    first_lane = lax.axis_index("seq") % (HD // QROWS) * QROWS
    return combine(names, first_lane.reshape(1).astype(jnp.int32), back, local_out, local_lse)


def solution(mesh):
    return jax.shard_map(
        local,
        mesh=mesh,
        in_specs=(
            P(("prefix", "seq"), None, None),
            P(("prefix", "seq"), None, None),
            P(("prefix", "seq"), None, None),
            P(("prefix", "seq"), None, None),
            P(("prefix", "seq"), None, None),
            P(("prefix", "seq")),
            P(("prefix", "seq"), None),
            P("prefix", "seq", None),
            P("prefix", "seq", None),
            P("prefix", "seq", None),
            P(),
        ),
        out_specs=P(("prefix", "seq"), None, None),
        check_vma=False,
    )
```

```python
import functools
import math

import jax
import jax.numpy as jnp
from jax import lax
from jax.experimental import pallas as pl
from jax.experimental.pallas import tpu as pltpu
from jax.sharding import PartitionSpec as P

QH = 64
KVH = 8
HD = 128
STEPS = 4
BLOCK = 128
GROUP = QH // KVH
QROWS = GROUP * STEPS
SLOTS = 2
PASSES = 2
PIECES = 2
TQ = 256
EXTRA = 8
SCALE = HD**-0.5
SCALE2 = SCALE * math.log2(math.e)
LN2 = math.log(2.0)
FLOOR = -1e30
NT = (((1,), (1,)), ((), ()))
MIB = 2**20


def arrange(rows):
    wide = rows.astype(jnp.float32)
    heads = []
    for k in range(KVH):
        parts = [wide[:, (k * GROUP + g) * HD : (k * GROUP + g + 1) * HD] for g in range(GROUP)]
        heads.append(jnp.concatenate(parts, axis=0))
    return heads


def slot_of_row(names, row, rows):
    prefix = names[row]
    seen = jnp.int32(0)
    for r in range(rows):
        earlier = jnp.logical_and(names[r] == prefix, r < row)
        seen = seen + earlier.astype(jnp.int32)
    return prefix, seen


def slot_index(prefix, slot):
    return (prefix // 2) * (2 * SLOTS) + slot * 2 + prefix % 2


def outgoing_kernel(names, q_ref, o_ref, a_ref):
    rows = q_ref.shape[0]
    o_ref[...] = jnp.zeros_like(o_ref)
    for r in range(rows):
        prefix, slot = slot_of_row(names, r, rows)
        place = slot_index(prefix, slot)
        heads = arrange(q_ref[r])
        for k in range(KVH):
            head = heads[k].astype(jnp.bfloat16)
            o_ref[place, k] = head
            a_ref[r, k] = head


def outgoing_queries(names, queries):
    slots = 8 * SLOTS
    return pl.pallas_call(
        outgoing_kernel,
        in_specs=[
            pl.BlockSpec(memory_space=pltpu.SMEM),
            pl.BlockSpec(memory_space=pltpu.VMEM),
        ],
        out_specs=[pl.BlockSpec(memory_space=pltpu.VMEM)] * 2,
        out_shape=[
            jax.ShapeDtypeStruct((slots, KVH, QROWS, HD), jnp.bfloat16),
            jax.ShapeDtypeStruct((queries.shape[0], KVH, QROWS, HD), jnp.bfloat16),
        ],
        cost_estimate=pl.CostEstimate(flops=0, bytes_accessed=2 * MIB, transcendentals=0),
    )(names, queries)


def prepare_kernel(core_ref, mine_ref, other_ref, table_ref, k_ref, v_ref, got_ref, o_ref):
    head = pl.program_id(0)
    core = core_ref[0]
    blocks = o_ref.shape[3] // BLOCK
    for source in range(2):
        place = core if source == 0 else 1 - core
        index_ref = mine_ref if source == 0 else other_ref
        for kind in range(2):
            for i in range(blocks):
                tokens = pl.ds(i * BLOCK, BLOCK)
                scale = table_ref[kind, index_ref[core * blocks + i, head]]
                if source == 0:
                    codes = (k_ref, v_ref)[kind][0, tokens, :]
                else:
                    codes = got_ref[kind, tokens, :]
                scaled = codes.astype(jnp.float32) * scale
                if kind == 1:
                    scaled = scaled.T
                o_ref[place, 0, kind, tokens] = scaled.astype(jnp.bfloat16)


def prepare(core, index, other_index, table, key_codes, value_codes, received):
    half = key_codes.shape[1] // 2
    smem = pl.BlockSpec(memory_space=pltpu.SMEM)
    codes = pl.BlockSpec((1, half, HD), lambda k, core: (0, core[0], k))
    return pl.pallas_call(
        prepare_kernel,
        grid_spec=pltpu.PrefetchScalarGridSpec(
            num_scalar_prefetch=1,
            grid=(KVH,),
            in_specs=[smem] * 3
            + [codes, codes, pl.BlockSpec((2, half, HD), lambda k, core: (0, 0, k))],
            out_specs=pl.BlockSpec((2, 1, 2, half, HD), lambda k, core: (0, k, 0, 0, 0)),
        ),
        out_shape=jax.ShapeDtypeStruct((2, KVH, 2, half, HD), jnp.bfloat16),
        cost_estimate=pl.CostEstimate(flops=0, bytes_accessed=12 * MIB, transcendentals=0),
    )(core, index, other_index, table, key_codes, value_codes, received)


def attend_kernel(first, last, *refs):
    refs = list(refs)
    q_ref, kv_ref = refs[:2]
    refs = refs[2:]
    before_ref = None if first else refs.pop(0)
    if last:
        out_ref = refs.pop(0)
        sa, sb, ma, mb, mid_ref = refs
    else:
        mid_ref, sa, sb, ma, mb = refs
    total = q_ref.shape[0]
    tiles = total // TQ
    sources, _, part, _ = kv_ref.shape
    run = sources // PASSES
    span = run * part

    def finish(turn, tile, both, top):
        columns = pl.ds(pl.multiple_of(tile * TQ, TQ), TQ)
        acc, sums = both[:HD], both[HD : HD + 8]
        if turn > 0 or not first:
            old_ref = mid_ref if turn > 0 else before_ref
            old_top = old_ref[HD + 8 :, columns]
            joint = jnp.maximum(old_top, top)
            old, new = jnp.exp2(old_top - joint), jnp.exp2(top - joint)
            acc = acc * new[:1] + old_ref[:HD, columns] * old[:1]
            sums = sums * new + old_ref[HD : HD + 8, columns] * old
            top = joint
        if turn < PASSES - 1 or not last:
            mid_ref[:HD, columns] = acc
            mid_ref[HD : HD + 8, columns] = sums
            mid_ref[HD + 8 :, columns] = top
            return
        out = (acc * (1.0 / sums[:1])).T.astype(jnp.bfloat16)
        lse = (top + jnp.log2(sums)) * LN2
        high = lse.astype(jnp.bfloat16).astype(jnp.float32)
        middle = (lse - high).astype(jnp.bfloat16).astype(jnp.float32)
        low = lse - high - middle
        line = lax.broadcasted_iota(jnp.int32, (EXTRA, TQ), 0)
        parts = jnp.where(line == 0, high, jnp.where(line == 1, middle, low)).astype(jnp.bfloat16)
        slots = TQ // QROWS
        out_ref[pl.ds(tile * slots, slots), :QROWS] = out.reshape(slots, QROWS, HD)
        for n in range(slots):
            lanes = n * QROWS // HD * HD
            out_ref[tile * slots + n, QROWS:] = parts[:, lanes : lanes + HD]

    def stage(score, weigh, s1, m1, s2, m2):
        if weigh:
            top = jnp.broadcast_to(jnp.max(m2[...], axis=0, keepdims=True) * SCALE2, (8, TQ))
        if score:
            q = q_ref[pl.ds(pl.multiple_of(score[1] * TQ, TQ), TQ), :]
            best = None
        both = None
        step = run // PIECES
        piece = step * part
        for n in range(PIECES):
            tokens = pl.ds(n * piece, piece)
            if score:
                keys = kv_ref[pl.ds(score[0] * run + n * step, step), 0].reshape(piece, HD)
                s = lax.dot_general(keys, q, NT, preferred_element_type=jnp.float32)
                s1[tokens, :] = s
                high = jnp.max(s.reshape(piece // 8, 8, TQ), axis=0)
                best = high if best is None else jnp.maximum(best, high)
            if weigh:
                weights = jnp.exp2(s2[tokens, :] * SCALE2 - top[:1]).astype(jnp.bfloat16)
                values = [
                    kv_ref[weigh[0] * run + n * step + j, 1, pl.ds(i * BLOCK, BLOCK), :]
                    for j in range(step)
                    for i in range(part // BLOCK)
                ]
                values = jnp.concatenate(values, axis=1)
                values = jnp.concatenate([values, jnp.ones((16, piece), jnp.bfloat16)], axis=0)
                more = jnp.dot(values, weights, preferred_element_type=jnp.float32)
                both = more if both is None else both + more
        if score:
            m1[...] = best
        if weigh:
            finish(weigh[0], weigh[1], both, top)

    stage((0, 0), None, sa, ma, sb, mb)
    for turn in range(PASSES):

        def double(g, carry):
            stage((turn, 2 * g + 1), (turn, 2 * g), sb, mb, sa, ma)
            stage((turn, 2 * g + 2), (turn, 2 * g + 1), sa, ma, sb, mb)
            return carry

        lax.fori_loop(0, tiles // 2 - 1, double, 0)
        stage((turn, tiles - 1), (turn, tiles - 2), sb, mb, sa, ma)
        following = (turn + 1, 0) if turn + 1 < PASSES else None
        stage(following, (turn, tiles - 1), sa, ma, sb, mb)


def attend(first, last, q, kv, state):
    total = q.shape[0]
    vmem = pl.BlockSpec(memory_space=pltpu.VMEM)
    tokens = kv.shape[0] * kv.shape[2]
    scratch = [pltpu.VMEM((tokens // PASSES, TQ), jnp.float32)] * 2
    scratch += [pltpu.VMEM((8, TQ), jnp.float32)] * 2
    held = (HD + 16, total)
    if last:
        shape = jax.ShapeDtypeStruct((total // QROWS, QROWS + EXTRA, HD), jnp.bfloat16)
        scratch.append(pltpu.VMEM(held, jnp.float32))
    else:
        shape = jax.ShapeDtypeStruct(held, jnp.float32)
    return pl.pallas_call(
        functools.partial(attend_kernel, first, last),
        in_specs=[vmem] * (2 + len(state)),
        out_specs=vmem,
        out_shape=shape,
        scratch_shapes=scratch,
        compiler_params=pltpu.CompilerParams(vmem_limit_bytes=40 * MIB),
        cost_estimate=pl.CostEstimate(
            flops=8 * total * tokens * HD, bytes_accessed=4 * MIB, transcendentals=total * tokens
        ),
    )(q, kv, *state)


def local_kernel(lens, q_ref, nk_ref, nv_ref, sk_ref, sv_ref, o_ref, l_ref):
    length = lens[pl.program_id(0)]
    suffix = sk_ref.shape[1]
    new_keys = nk_ref[0].astype(jnp.float32)
    new_values = nv_ref[0].astype(jnp.float32)
    pad = jnp.zeros((GROUP * 2 - STEPS, HD), jnp.float32)
    visible = lax.broadcasted_iota(jnp.int32, (QROWS, suffix), 1) < length
    step = lax.broadcasted_iota(jnp.int32, (QROWS, 2 * GROUP), 0) % STEPS
    fresh = lax.broadcasted_iota(jnp.int32, (QROWS, 2 * GROUP), 1) <= step
    for k in range(KVH):
        lanes = slice(k * HD, (k + 1) * HD)
        q = q_ref[0, k]
        nk = jnp.concatenate([new_keys[:, lanes], pad], axis=0).astype(jnp.bfloat16)
        nv = jnp.concatenate([new_values[:, lanes], pad], axis=0).astype(jnp.bfloat16)
        s = lax.dot_general(q, sk_ref[0, :, lanes], NT, preferred_element_type=jnp.float32)
        n = lax.dot_general(q, nk, NT, preferred_element_type=jnp.float32)
        s = jnp.where(visible, s * SCALE, FLOOR)
        n = jnp.where(fresh, n * SCALE, FLOOR)
        top = jnp.maximum(jnp.max(s, axis=1, keepdims=True), jnp.max(n, axis=1, keepdims=True))
        es, en = jnp.exp(s - top), jnp.exp(n - top)
        sums = jnp.sum(es, axis=1, keepdims=True) + jnp.sum(en, axis=1, keepdims=True)
        out = jnp.dot(
            es.astype(jnp.bfloat16), sv_ref[0, :, lanes], preferred_element_type=jnp.float32
        ) + jnp.dot(en.astype(jnp.bfloat16), nv, preferred_element_type=jnp.float32)
        o_ref[0, k] = out / sums
        l_ref[0, k] = jnp.broadcast_to(top + jnp.log(sums), (QROWS, HD))


def local_attention(lens, queries, new_keys, new_values, suffix_keys, suffix_values):
    rows, suffix, width = suffix_keys.shape

    def by_row(*shape):
        return pl.BlockSpec((1,) + shape, lambda r, lens: (r,) + (0,) * len(shape))

    return pl.pallas_call(
        local_kernel,
        grid_spec=pltpu.PrefetchScalarGridSpec(
            num_scalar_prefetch=1,
            grid=(rows,),
            in_specs=[
                by_row(KVH, QROWS, HD),
                by_row(STEPS, width),
                by_row(STEPS, width),
                by_row(suffix, width),
                by_row(suffix, width),
            ],
            out_specs=[by_row(KVH, QROWS, HD)] * 2,
        ),
        out_shape=[pltpu.HBM((rows, KVH, QROWS, HD), jnp.float32)] * 2,
        compiler_params=pltpu.CompilerParams(vmem_limit_bytes=24 * MIB),
        cost_estimate=pl.CostEstimate(
            flops=4 * rows * QH * STEPS * suffix * HD,
            bytes_accessed=10 * MIB,
            transcendentals=rows * QH * STEPS * suffix,
        ),
    )(lens, queries, new_keys, new_values, in_hbm(suffix_keys), in_hbm(suffix_values))


def combine_kernel(names, first_lane, back_ref, out_ref, lse_ref, o_ref):
    rows = out_ref.shape[0]
    lane = lax.broadcasted_iota(jnp.int32, (QROWS, HD), 1)
    row = lax.broadcasted_iota(jnp.int32, (QROWS, HD), 0)
    mine = lane == row + first_lane[0]

    def mix(r, carry):
        prefix, slot = slot_of_row(names, r, rows)
        place = slot_index(prefix, slot)
        for k in range(KVH):
            prefix_out = back_ref[place, k, :QROWS].astype(jnp.float32)
            parts = back_ref[place, k, QROWS:].astype(jnp.float32)
            spread = jnp.where(mine, parts[:1] + parts[1:2] + parts[2:3], 0.0)
            prefix_lse = jnp.sum(spread, axis=1, keepdims=True)
            local_lse = lse_ref[r, k]
            joint = jnp.maximum(local_lse, prefix_lse)
            local_share = jnp.exp(local_lse - joint)
            prefix_share = jnp.exp(prefix_lse - joint)
            mixed = (local_share * out_ref[r, k] + prefix_share * prefix_out) / (
                local_share + prefix_share
            )
            for g in range(GROUP):
                o_ref[r, :, (k * GROUP + g) * HD : (k * GROUP + g + 1) * HD] = mixed[
                    g * STEPS : (g + 1) * STEPS
                ].astype(jnp.bfloat16)
        return carry

    lax.fori_loop(0, rows, mix, 0)


def in_hbm(x):
    return pltpu.with_memory_space_constraint(x, pltpu.HBM)


def combine(names, first_lane, back, local_out, local_lse):
    rows = local_out.shape[0]
    vmem = pl.BlockSpec(memory_space=pltpu.VMEM)
    return pl.pallas_call(
        combine_kernel,
        in_specs=[pl.BlockSpec(memory_space=pltpu.SMEM)] * 2 + [vmem] * 3,
        out_specs=vmem,
        out_shape=jax.ShapeDtypeStruct((rows, STEPS, QH * HD), jnp.bfloat16),
        compiler_params=pltpu.CompilerParams(vmem_limit_bytes=16 * MIB),
        cost_estimate=pl.CostEstimate(flops=0, bytes_accessed=4 * MIB, transcendentals=0),
    )(names, first_lane, back, in_hbm(local_out), in_hbm(local_lse))


def local(
    queries,
    new_keys,
    new_values,
    suffix_keys,
    suffix_values,
    suffix_len,
    row_prefix,
    prefix_key_codes,
    prefix_value_codes,
    scale_index,
    scale_table,
):
    groups = lax.axis_size("prefix")
    shards = lax.axis_size("seq")
    core = lax.axis_index("prefix") % 2
    swap = [(i, i ^ 1) for i in range(groups)]
    names = row_prefix[:, 0]

    half = prefix_key_codes.shape[1] // 2
    sent = [
        lax.dynamic_slice_in_dim(codes[0], (1 - core) * half, half, 0)
        for codes in (prefix_key_codes, prefix_value_codes)
    ]
    received = lax.ppermute(jnp.stack(sent), "prefix", swap)
    other_index = lax.ppermute(scale_index, "prefix", swap)
    outgoing, arranged = outgoing_queries(names, queries)
    arrived = lax.all_to_all(
        outgoing.reshape(groups * shards, QROWS, HD),
        ("prefix", "seq"),
        split_axis=0,
        concat_axis=0,
        tiled=True,
    )
    q = arrived.reshape(-1, HD)
    moved = prepare(
        core.reshape(1).astype(jnp.int32),
        scale_index[0],
        other_index[0],
        scale_table,
        prefix_key_codes,
        prefix_value_codes,
        received,
    ).reshape(2 * KVH, 2, half, HD)
    moved, q = lax.optimization_barrier((moved, q))
    own = lax.all_to_all(moved, "seq", split_axis=0, concat_axis=0, tiled=True)
    other = lax.ppermute(own, "prefix", swap)
    state = attend(True, False, q, own, ())
    answer = attend(False, True, q, other, (state,))
    local_out, local_lse = local_attention(
        suffix_len, arranged, new_keys, new_values, suffix_keys, suffix_values
    )
    back = lax.all_to_all(answer, ("prefix", "seq"), split_axis=0, concat_axis=0, tiled=True)
    back = back.reshape(groups * SLOTS, KVH, QROWS + EXTRA, HD)
    first_lane = lax.axis_index("seq") % (HD // QROWS) * QROWS
    return combine(names, first_lane.reshape(1).astype(jnp.int32), back, local_out, local_lse)


def solution(mesh):
    return jax.shard_map(
        local,
        mesh=mesh,
        in_specs=(
            P(("prefix", "seq"), None, None),
            P(("prefix", "seq"), None, None),
            P(("prefix", "seq"), None, None),
            P(("prefix", "seq"), None, None),
            P(("prefix", "seq"), None, None),
            P(("prefix", "seq")),
            P(("prefix", "seq"), None),
            P("prefix", "seq", None),
            P("prefix", "seq", None),
            P("prefix", "seq", None),
            P(),
        ),
        out_specs=P(("prefix", "seq"), None, None),
        check_vma=False,
    )
```

```python
import functools
import math

import jax
import jax.numpy as jnp
from jax import lax
from jax.experimental import pallas as pl
from jax.experimental.pallas import tpu as pltpu
from jax.sharding import PartitionSpec as P

QH = 64
KVH = 8
HD = 128
STEPS = 4
BLOCK = 128
GROUP = QH // KVH
QROWS = GROUP * STEPS
SLOTS = 2
PASSES = 2
PIECES = 2
TQ = 256
EXTRA = 8
SCALE = HD**-0.5
SCALE2 = SCALE * math.log2(math.e)
LN2 = math.log(2.0)
FLOOR = -1e30
NT = (((1,), (1,)), ((), ()))
MIB = 2**20


def arrange(rows):
    wide = rows.astype(jnp.float32)
    heads = []
    for k in range(KVH):
        parts = [wide[:, (k * GROUP + g) * HD : (k * GROUP + g + 1) * HD] for g in range(GROUP)]
        heads.append(jnp.concatenate(parts, axis=0))
    return heads


def slot_of_row(names, row, rows):
    prefix = names[row]
    seen = jnp.int32(0)
    for r in range(rows):
        earlier = jnp.logical_and(names[r] == prefix, r < row)
        seen = seen + earlier.astype(jnp.int32)
    return prefix, seen


def slot_index(prefix, slot):
    return (prefix // 2) * (2 * SLOTS) + slot * 2 + prefix % 2


def outgoing_kernel(names, q_ref, o_ref, a_ref):
    rows = q_ref.shape[0]
    o_ref[...] = jnp.zeros_like(o_ref)
    for r in range(rows):
        prefix, slot = slot_of_row(names, r, rows)
        place = slot_index(prefix, slot)
        heads = arrange(q_ref[r])
        for k in range(KVH):
            head = heads[k].astype(jnp.bfloat16)
            o_ref[place, k] = head
            a_ref[r, k] = head


def outgoing_queries(names, queries):
    slots = 8 * SLOTS
    return pl.pallas_call(
        outgoing_kernel,
        in_specs=[
            pl.BlockSpec(memory_space=pltpu.SMEM),
            pl.BlockSpec(memory_space=pltpu.VMEM),
        ],
        out_specs=[pl.BlockSpec(memory_space=pltpu.VMEM)] * 2,
        out_shape=[
            jax.ShapeDtypeStruct((slots, KVH, QROWS, HD), jnp.bfloat16),
            jax.ShapeDtypeStruct((queries.shape[0], KVH, QROWS, HD), jnp.bfloat16),
        ],
        cost_estimate=pl.CostEstimate(flops=0, bytes_accessed=2 * MIB, transcendentals=0),
    )(names, queries)


def prepare_kernel(core_ref, mine_ref, other_ref, table_ref, k_ref, v_ref, got_ref, o_ref):
    head = pl.program_id(0)
    core = core_ref[0]
    blocks = o_ref.shape[3] // BLOCK
    for source in range(2):
        place = core if source == 0 else 1 - core
        index_ref = mine_ref if source == 0 else other_ref
        for kind in range(2):
            for i in range(blocks):
                tokens = pl.ds(i * BLOCK, BLOCK)
                scale = table_ref[kind, index_ref[core * blocks + i, head]]
                if source == 0:
                    codes = (k_ref, v_ref)[kind][0, tokens, :]
                else:
                    codes = got_ref[kind, tokens, :]
                scaled = codes.astype(jnp.float32) * scale
                if kind == 1:
                    scaled = scaled.T
                o_ref[place, 0, kind, tokens] = scaled.astype(jnp.bfloat16)


def prepare(core, index, other_index, table, key_codes, value_codes, received):
    half = key_codes.shape[1] // 2
    smem = pl.BlockSpec(memory_space=pltpu.SMEM)
    codes = pl.BlockSpec((1, half, HD), lambda k, core: (0, core[0], k))
    return pl.pallas_call(
        prepare_kernel,
        grid_spec=pltpu.PrefetchScalarGridSpec(
            num_scalar_prefetch=1,
            grid=(KVH,),
            in_specs=[smem] * 3
            + [codes, codes, pl.BlockSpec((2, half, HD), lambda k, core: (0, 0, k))],
            out_specs=pl.BlockSpec((2, 1, 2, half, HD), lambda k, core: (0, k, 0, 0, 0)),
        ),
        out_shape=jax.ShapeDtypeStruct((2, KVH, 2, half, HD), jnp.bfloat16),
        cost_estimate=pl.CostEstimate(flops=0, bytes_accessed=12 * MIB, transcendentals=0),
    )(core, index, other_index, table, key_codes, value_codes, received)


def attend_kernel(first, last, *refs):
    refs = list(refs)
    q_ref, kv_ref = refs[:2]
    refs = refs[2:]
    before_ref = None if first else refs.pop(0)
    if last:
        out_ref = refs.pop(0)
        sa, sb, ma, mb, mid_ref = refs
    else:
        mid_ref, sa, sb, ma, mb = refs
    total = q_ref.shape[0]
    tiles = total // TQ
    sources, _, part, _ = kv_ref.shape
    run = sources // PASSES
    span = run * part

    def finish(turn, tile, both, top):
        columns = pl.ds(pl.multiple_of(tile * TQ, TQ), TQ)
        acc, sums = both[:HD], both[HD : HD + 8]
        if turn > 0 or not first:
            old_ref = mid_ref if turn > 0 else before_ref
            old_top = old_ref[HD + 8 :, columns]
            joint = jnp.maximum(old_top, top)
            old, new = jnp.exp2(old_top - joint), jnp.exp2(top - joint)
            acc = acc * new[:1] + old_ref[:HD, columns] * old[:1]
            sums = sums * new + old_ref[HD : HD + 8, columns] * old
            top = joint
        if turn < PASSES - 1 or not last:
            mid_ref[:HD, columns] = acc
            mid_ref[HD : HD + 8, columns] = sums
            mid_ref[HD + 8 :, columns] = top
            return
        out = (acc * (1.0 / sums[:1])).T.astype(jnp.bfloat16)
        lse = (top + jnp.log2(sums)) * LN2
        high = lse.astype(jnp.bfloat16).astype(jnp.float32)
        middle = (lse - high).astype(jnp.bfloat16).astype(jnp.float32)
        low = lse - high - middle
        line = lax.broadcasted_iota(jnp.int32, (EXTRA, TQ), 0)
        parts = jnp.where(line == 0, high, jnp.where(line == 1, middle, low)).astype(jnp.bfloat16)
        slots = TQ // QROWS
        out_ref[pl.ds(tile * slots, slots), :QROWS] = out.reshape(slots, QROWS, HD)
        for n in range(slots):
            lanes = n * QROWS // HD * HD
            out_ref[tile * slots + n, QROWS:] = parts[:, lanes : lanes + HD]

    def stage(score, weigh, s1, m1, s2, m2):
        if weigh:
            top = jnp.broadcast_to(jnp.max(m2[...], axis=0, keepdims=True) * SCALE2, (8, TQ))
        if score:
            q = q_ref[pl.ds(pl.multiple_of(score[1] * TQ, TQ), TQ), :]
            best = None
        both = None
        step = run // PIECES
        piece = step * part
        for n in range(PIECES):
            tokens = pl.ds(n * piece, piece)
            if score:
                keys = kv_ref[pl.ds(score[0] * run + n * step, step), 0].reshape(piece, HD)
                s = lax.dot_general(keys, q, NT, preferred_element_type=jnp.float32)
                s1[tokens, :] = s
                high = jnp.max(s.reshape(piece // 8, 8, TQ), axis=0)
                best = high if best is None else jnp.maximum(best, high)
            if weigh:
                weights = jnp.exp2(s2[tokens, :] * SCALE2 - top[:1]).astype(jnp.bfloat16)
                values = [
                    kv_ref[weigh[0] * run + n * step + j, 1, pl.ds(i * BLOCK, BLOCK), :]
                    for j in range(step)
                    for i in range(part // BLOCK)
                ]
                values = jnp.concatenate(values, axis=1)
                values = jnp.concatenate([values, jnp.ones((16, piece), jnp.bfloat16)], axis=0)
                more = jnp.dot(values, weights, preferred_element_type=jnp.float32)
                both = more if both is None else both + more
        if score:
            m1[...] = best
        if weigh:
            finish(weigh[0], weigh[1], both, top)

    stage((0, 0), None, sa, ma, sb, mb)
    for turn in range(PASSES):

        def double(g, carry):
            stage((turn, 2 * g + 1), (turn, 2 * g), sb, mb, sa, ma)
            stage((turn, 2 * g + 2), (turn, 2 * g + 1), sa, ma, sb, mb)
            return carry

        lax.fori_loop(0, tiles // 2 - 1, double, 0)
        stage((turn, tiles - 1), (turn, tiles - 2), sb, mb, sa, ma)
        following = (turn + 1, 0) if turn + 1 < PASSES else None
        stage(following, (turn, tiles - 1), sa, ma, sb, mb)


def attend(first, last, q, kv, state):
    total = q.shape[0]
    vmem = pl.BlockSpec(memory_space=pltpu.VMEM)
    tokens = kv.shape[0] * kv.shape[2]
    scratch = [pltpu.VMEM((tokens // PASSES, TQ), jnp.float32)] * 2
    scratch += [pltpu.VMEM((8, TQ), jnp.float32)] * 2
    held = (HD + 16, total)
    if last:
        shape = jax.ShapeDtypeStruct((total // QROWS, QROWS + EXTRA, HD), jnp.bfloat16)
        scratch.append(pltpu.VMEM(held, jnp.float32))
    else:
        shape = jax.ShapeDtypeStruct(held, jnp.float32)
    return pl.pallas_call(
        functools.partial(attend_kernel, first, last),
        in_specs=[vmem] * (2 + len(state)),
        out_specs=vmem,
        out_shape=shape,
        scratch_shapes=scratch,
        compiler_params=pltpu.CompilerParams(vmem_limit_bytes=40 * MIB),
        cost_estimate=pl.CostEstimate(
            flops=8 * total * tokens * HD, bytes_accessed=4 * MIB, transcendentals=total * tokens
        ),
    )(q, kv, *state)


def local_kernel(lens, q_ref, nk_ref, nv_ref, sk_ref, sv_ref, o_ref, l_ref):
    length = lens[pl.program_id(0)]
    suffix = sk_ref.shape[1]
    new_keys = nk_ref[0].astype(jnp.float32)
    new_values = nv_ref[0].astype(jnp.float32)
    pad = jnp.zeros((GROUP * 2 - STEPS, HD), jnp.float32)
    visible = lax.broadcasted_iota(jnp.int32, (QROWS, suffix), 1) < length
    step = lax.broadcasted_iota(jnp.int32, (QROWS, 2 * GROUP), 0) % STEPS
    fresh = lax.broadcasted_iota(jnp.int32, (QROWS, 2 * GROUP), 1) <= step
    for k in range(KVH):
        lanes = slice(k * HD, (k + 1) * HD)
        q = q_ref[0, k]
        nk = jnp.concatenate([new_keys[:, lanes], pad], axis=0).astype(jnp.bfloat16)
        nv = jnp.concatenate([new_values[:, lanes], pad], axis=0).astype(jnp.bfloat16)
        s = lax.dot_general(q, sk_ref[0, :, lanes], NT, preferred_element_type=jnp.float32)
        n = lax.dot_general(q, nk, NT, preferred_element_type=jnp.float32)
        s = jnp.where(visible, s * SCALE, FLOOR)
        n = jnp.where(fresh, n * SCALE, FLOOR)
        top = jnp.maximum(jnp.max(s, axis=1, keepdims=True), jnp.max(n, axis=1, keepdims=True))
        es, en = jnp.exp(s - top), jnp.exp(n - top)
        sums = jnp.sum(es, axis=1, keepdims=True) + jnp.sum(en, axis=1, keepdims=True)
        out = jnp.dot(
            es.astype(jnp.bfloat16), sv_ref[0, :, lanes], preferred_element_type=jnp.float32
        ) + jnp.dot(en.astype(jnp.bfloat16), nv, preferred_element_type=jnp.float32)
        o_ref[0, k] = out / sums
        l_ref[0, k] = jnp.broadcast_to(top + jnp.log(sums), (QROWS, HD))


def local_attention(lens, queries, new_keys, new_values, suffix_keys, suffix_values):
    rows, suffix, width = suffix_keys.shape

    def by_row(*shape):
        return pl.BlockSpec((1,) + shape, lambda r, lens: (r,) + (0,) * len(shape))

    return pl.pallas_call(
        local_kernel,
        grid_spec=pltpu.PrefetchScalarGridSpec(
            num_scalar_prefetch=1,
            grid=(rows,),
            in_specs=[
                by_row(KVH, QROWS, HD),
                by_row(STEPS, width),
                by_row(STEPS, width),
                by_row(suffix, width),
                by_row(suffix, width),
            ],
            out_specs=[by_row(KVH, QROWS, HD)] * 2,
        ),
        out_shape=[pltpu.HBM((rows, KVH, QROWS, HD), jnp.float32)] * 2,
        compiler_params=pltpu.CompilerParams(vmem_limit_bytes=24 * MIB),
        cost_estimate=pl.CostEstimate(
            flops=4 * rows * QH * STEPS * suffix * HD,
            bytes_accessed=10 * MIB,
            transcendentals=rows * QH * STEPS * suffix,
        ),
    )(lens, queries, new_keys, new_values, in_hbm(suffix_keys), in_hbm(suffix_values))


def combine_kernel(names, first_lane, back_ref, out_ref, lse_ref, o_ref):
    rows = out_ref.shape[0]
    lane = lax.broadcasted_iota(jnp.int32, (QROWS, HD), 1)
    row = lax.broadcasted_iota(jnp.int32, (QROWS, HD), 0)
    mine = lane == row + first_lane[0]

    def mix(r, carry):
        prefix, slot = slot_of_row(names, r, rows)
        place = slot_index(prefix, slot)
        for k in range(KVH):
            prefix_out = back_ref[place, k, :QROWS].astype(jnp.float32)
            parts = back_ref[place, k, QROWS:].astype(jnp.float32)
            spread = jnp.where(mine, parts[:1] + parts[1:2] + parts[2:3], 0.0)
            prefix_lse = jnp.sum(spread, axis=1, keepdims=True)
            local_lse = lse_ref[r, k]
            joint = jnp.maximum(local_lse, prefix_lse)
            local_share = jnp.exp(local_lse - joint)
            prefix_share = jnp.exp(prefix_lse - joint)
            mixed = (local_share * out_ref[r, k] + prefix_share * prefix_out) / (
                local_share + prefix_share
            )
            for g in range(GROUP):
                o_ref[r, :, (k * GROUP + g) * HD : (k * GROUP + g + 1) * HD] = mixed[
                    g * STEPS : (g + 1) * STEPS
                ].astype(jnp.bfloat16)
        return carry

    lax.fori_loop(0, rows, mix, 0, unroll=2)


def in_hbm(x):
    return pltpu.with_memory_space_constraint(x, pltpu.HBM)


def combine(names, first_lane, back, local_out, local_lse):
    rows = local_out.shape[0]
    vmem = pl.BlockSpec(memory_space=pltpu.VMEM)
    return pl.pallas_call(
        combine_kernel,
        in_specs=[pl.BlockSpec(memory_space=pltpu.SMEM)] * 2 + [vmem] * 3,
        out_specs=vmem,
        out_shape=jax.ShapeDtypeStruct((rows, STEPS, QH * HD), jnp.bfloat16),
        compiler_params=pltpu.CompilerParams(vmem_limit_bytes=16 * MIB),
        cost_estimate=pl.CostEstimate(flops=0, bytes_accessed=4 * MIB, transcendentals=0),
    )(names, first_lane, back, in_hbm(local_out), in_hbm(local_lse))


def local(
    queries,
    new_keys,
    new_values,
    suffix_keys,
    suffix_values,
    suffix_len,
    row_prefix,
    prefix_key_codes,
    prefix_value_codes,
    scale_index,
    scale_table,
):
    groups = lax.axis_size("prefix")
    shards = lax.axis_size("seq")
    core = lax.axis_index("prefix") % 2
    swap = [(i, i ^ 1) for i in range(groups)]
    names = row_prefix[:, 0]

    half = prefix_key_codes.shape[1] // 2
    sent = [
        lax.dynamic_slice_in_dim(codes[0], (1 - core) * half, half, 0)
        for codes in (prefix_key_codes, prefix_value_codes)
    ]
    received = lax.ppermute(jnp.stack(sent), "prefix", swap)
    other_index = lax.ppermute(scale_index, "prefix", swap)
    outgoing, arranged = outgoing_queries(names, queries)
    arrived = lax.all_to_all(
        outgoing.reshape(groups * shards, QROWS, HD),
        ("prefix", "seq"),
        split_axis=0,
        concat_axis=0,
        tiled=True,
    )
    q = arrived.reshape(-1, HD)
    moved = prepare(
        core.reshape(1).astype(jnp.int32),
        scale_index[0],
        other_index[0],
        scale_table,
        prefix_key_codes,
        prefix_value_codes,
        received,
    ).reshape(2 * KVH, 2, half, HD)
    moved, q = lax.optimization_barrier((moved, q))
    own = lax.all_to_all(moved, "seq", split_axis=0, concat_axis=0, tiled=True)
    other = lax.ppermute(own, "prefix", swap)
    state = attend(True, False, q, own, ())
    answer = attend(False, True, q, other, (state,))
    local_out, local_lse = local_attention(
        suffix_len, arranged, new_keys, new_values, suffix_keys, suffix_values
    )
    back = lax.all_to_all(answer, ("prefix", "seq"), split_axis=0, concat_axis=0, tiled=True)
    back = back.reshape(groups * SLOTS, KVH, QROWS + EXTRA, HD)
    first_lane = lax.axis_index("seq") % (HD // QROWS) * QROWS
    return combine(names, first_lane.reshape(1).astype(jnp.int32), back, local_out, local_lse)


def solution(mesh):
    return jax.shard_map(
        local,
        mesh=mesh,
        in_specs=(
            P(("prefix", "seq"), None, None),
            P(("prefix", "seq"), None, None),
            P(("prefix", "seq"), None, None),
            P(("prefix", "seq"), None, None),
            P(("prefix", "seq"), None, None),
            P(("prefix", "seq")),
            P(("prefix", "seq"), None),
            P("prefix", "seq", None),
            P("prefix", "seq", None),
            P("prefix", "seq", None),
            P(),
        ),
        out_specs=P(("prefix", "seq"), None, None),
        check_vma=False,
    )
```
